32 devices in a mesh: row: 4 (over y, x), lmk: 4 (over z), bw: 2 (over core).
Axes of the slice: x: 2, y: 2, z: 4, core: 2. Of those that a mesh axis runs over, the one named last changes fastest.
Arguments:
- embeddings: bfloat16 [6144, 1024], P(('row', 'lmk')), may hold values from -6 to 6
- candidates: bfloat16 [32768, 1024], P(('row', 'lmk')), may hold values from -6 to 6
- block_owner: int32 [2], replicated, may hold values from 0 to 15, as said below
- landmark_picks: int32 [2, 2048], replicated, may hold values from 0 to 2047, each once within a row
- inverse_width: float32 [8], P('bw'), may hold values from 2 to 16
- mixture: float32 [8], P('bw'), may hold values from 0.05 to 0.25
- whitening: bfloat16 [4096, 4096], P(None, 'bw'), may hold values from -0.09375 to 0.09375
Outputs:
- features: bfloat16 [6144, 4096], P(('row', 'lmk'), 'bw')
The draws below stay inside these ranges and needn't reach their ends.
Inputs may be any that keep to these rules, and one draw needn't show every extreme that they name: `block_owner`: the 2 owners are different, and 15 is one of them. `landmark_picks`: each row is an ordering of 0 to 2047.
All inputs are finite; a program needn't handle non-finite values.
Results may differ from the reference program's by a relative error of at most 0.0055.
Values may be sent and summed in bfloat16 or wider, within the bound.
A program may use at most 128 MiB of HBM per device.

```python
import math
import jax
import jax.numpy as jnp
from jax import lax

D = 1024
BLK = 2048
NBLK = 2
NBW = 8
R_DEV = 384
M = 4096
OWNERS = 16
ROWS = 6144
POOL = 32768


def draw_block_owner(key, part):
    first_key, second_key = jax.random.split(key)
    other = jax.random.randint(first_key, (), 0, OWNERS - 1)
    flipped = jax.random.randint(second_key, (), 0, 2)
    highest = jnp.int32(OWNERS - 1)
    leading = jnp.where(flipped == 1, highest, other)
    trailing = jnp.where(flipped == 1, other, highest)
    return jnp.stack([leading, trailing]).astype(jnp.int32)


def levels(own_key, extent, cuts, smallest, largest):
    def one(axis_at, shards_of):
        steps = jax.random.uniform(jax.random.fold_in(jax.random.fold_in(own_key, 6), axis_at), (shards_of,), jnp.float32, smallest / len(cuts), largest / len(cuts))
        return jnp.repeat(jnp.exp(steps), extent[axis_at] // shards_of).reshape((-1,) + (1,) * (len(extent) - axis_at - 1))

    factor_of = one(*cuts[0])
    for cut in cuts[1:]:
        factor_of = factor_of * one(*cut)
    return factor_of


def bell_draw(own_key, shape, width, reach, pieces=(), kind=jnp.bfloat16):
    drawn = width * jax.random.normal(own_key, shape, jnp.float32)
    if pieces:
        drawn = drawn * levels(own_key, shape, pieces, -0.22, 0.18)
    return jnp.clip(drawn, -reach, reach).astype(kind)


def setup_inputs(seed: int = 0) -> dict:
    streams_of = jax.random.split(jax.random.key(seed), 8)
    embeddings = bell_draw(streams_of[0], (ROWS, D), 1.0, 6.0, ((0, 16),))
    candidates = bell_draw(streams_of[1], (POOL, D), 1.0, 6.0, ((0, 16),))
    block_owner = draw_block_owner(jax.random.fold_in(streams_of[7], 71), 0)
    landmark_picks = jax.vmap(lambda own: jax.random.permutation(own, BLK))(jax.random.split(streams_of[3], NBLK)).reshape((NBLK, BLK)).astype(jnp.int32)
    inverse_width = jnp.clip(jnp.exp(math.log(16.0) - 2.0794415 * jax.random.uniform(streams_of[4], (NBW,), jnp.float32) ** levels(streams_of[4], (NBW,), ((0, 2),), -0.2, 0.2)), 2.0, 16.0)
    mixture = jnp.clip(jnp.exp(math.log(0.25) - 1.609438 * jax.random.uniform(streams_of[5], (NBW,), jnp.float32) ** levels(streams_of[5], (NBW,), ((0, 2),), -0.2, 0.2)), 0.05, 0.25)
    whitening = bell_draw(streams_of[6], (M, M), M ** -0.5, 0.09375, ((1, 2),))
    return {"embeddings": embeddings, "candidates": candidates, "block_owner": block_owner, "landmark_picks": landmark_picks, "inverse_width": inverse_width, "mixture": mixture, "whitening": whitening}


def normalize(matrix_rows):
    widened = matrix_rows.astype(jnp.float32)
    scale = lax.rsqrt(lax.optimization_barrier(jnp.sum(widened * widened, axis=-1, keepdims=True)) + 1e-06)
    return (widened * scale).astype(jnp.bfloat16)

def kernel_of(cosine, widths, weights):
    running = jnp.zeros(cosine.shape, jnp.float32)
    for which in range(widths.shape[0]):
        running = running + weights[which] * jnp.exp(2.0 * widths[which] * cosine)
    return running

def reference(embeddings, candidates, block_owner, landmark_picks, inverse_width, mixture, whitening):
    unit_rows = normalize(embeddings)
    chosen_rows = (block_owner.astype(jnp.int32)[:, None] * BLK + landmark_picks.astype(jnp.int32)).reshape(-1)
    landmarks = normalize(jnp.take(candidates, chosen_rows, axis=0))

    def one_block(row_block):
        cosine = jnp.einsum('rd,md->rm', row_block, landmarks, preferred_element_type=jnp.float32)
        kernel = kernel_of(cosine, inverse_width, mixture).astype(jnp.bfloat16)
        return jnp.dot(kernel, whitening, preferred_element_type=jnp.float32).astype(jnp.bfloat16)
    grouped = unit_rows.reshape(ROWS // R_DEV, R_DEV, D)
    result = lax.map(one_block, grouped)
    return result.reshape(ROWS, M)
```

```python
import functools
import random

import jax
import jax.numpy as jnp
import numpy as np
from jax import lax
from jax.experimental import pallas as pl
from jax.experimental.pallas import tpu as pltpu
from jax.sharding import PartitionSpec as P

MESH = pl.DeviceIdType.MESH
TREES = 3
STEP_ROWS = 16


class Chips:
    def __init__(self, rows, lmks):
        self.rows, self.lmks = rows, lmks
        self.count = rows * lmks
        self.torus = rows != 4
        if self.torus:
            assert rows == 8 and lmks == 8
            self.back = (1, 0, 3, 2, 5, 4)
        else:
            self.back = (0, 1, 3, 2)
        self.links = len(self.back)

    def neighbour(self, link, row, lmk):
        if not self.torus:
            if link == 0:
                return (row + 2) % 4, lmk
            if link == 1:
                return row + 1 - 2 * (row % 2), lmk
            return row, lmk + (1 if link == 2 else -1)
        x, y, z = row % 4, lmk % 4, (row // 4) * 2 + lmk // 4
        step = 1 if link % 2 == 0 else 3
        if link // 2 == 0:
            x = (x + step) % 4
        elif link // 2 == 1:
            y = (y + step) % 4
        else:
            z = (z + step) % 4
        return (z // 2) * 4 + x, (z % 2) * 4 + y

    def present(self, link, lmk):
        if self.torus or link < 2:
            return None
        return lmk < self.lmks - 1 if link == 2 else lmk > 0

    def degree(self, lmk):
        if self.torus:
            return self.links
        return 2 + jnp.minimum(lmk, 1) + jnp.minimum(self.lmks - 1 - lmk, 1)

    def edges(self, chip):
        row, lmk = chip // self.lmks, chip % self.lmks
        for link in range(self.links):
            here = self.present(link, lmk)
            if here is None or here:
                r, k = self.neighbour(link, row, lmk)
                yield link, r * self.lmks + k


GRID_TREES = [
    [
        [0, 0, 1, 2, 5, 1, 2, 3, 9, 1, 2, 3, 13, 5, 13, 14],
        [0, 9, 10, 11, 12, 13, 14, 15, 0, 8, 9, 10, 8, 9, 10, 11],
        [0, 5, 6, 7, 0, 4, 5, 6, 12, 13, 14, 15, 4, 12, 6, 7],
    ],
    [
        [1, 1, 1, 2, 0, 4, 2, 3, 0, 10, 2, 3, 8, 14, 6, 7],
        [4, 1, 6, 7, 5, 1, 5, 6, 12, 13, 14, 15, 4, 5, 13, 14],
        [8, 1, 10, 11, 12, 13, 14, 15, 9, 1, 9, 10, 13, 9, 10, 11],
    ],
]


def torus_trees(chips):
    for seed in range(1000):
        draw = random.Random(seed)
        used, trees = set(), []
        for tree in range(TREES):
            parent, level = {0: 0}, [0]
            while level:
                following = []
                draw.shuffle(level)
                for chip in level:
                    for link, other in chips.edges(chip):
                        if other in parent or (chip, link) in used:
                            continue
                        if chip == 0 and link // 2 != tree:
                            continue
                        used.add((chip, link))
                        parent[other] = chip
                        following.append(other)
                level = following
            trees.append(parent)
        if all(len(parent) == chips.count for parent in trees):
            return [[parent[chip] for chip in range(chips.count)] for parent in trees]
    raise ValueError("no trees")


def moved(chips, owner):
    if not chips.torus:
        y, x, z = owner // 8, owner // 4 % 2, owner % 4
        turn = z >= 2
        image = [
            ((c // 8) ^ y) * 8 + ((c // 4 % 2) ^ x) * 4 + (3 - c % 4 if turn else c % 4)
            for c in range(16)
        ]
        return image, (3 - z if turn else z)

    def place(chip):
        row, lmk = chip // 8, chip % 8
        return row % 4, lmk % 4, (row // 4) * 2 + lmk // 4

    away = place(owner)
    image = []
    for chip in range(chips.count):
        x, y, z = ((a + b) % 4 for a, b in zip(place(chip), away))
        image.append(((z // 2) * 4 + x) * 8 + (z % 2) * 4 + y)
    return image, 0


@functools.lru_cache(maxsize=None)
def routes(rows, lmks):
    chips = Chips(rows, lmks)
    stored = [torus_trees(chips)] if chips.torus else GRID_TREES
    n = chips.count
    parent_link = np.full((n, n, TREES), -1, np.int32)
    depth = np.zeros((n, n, TREES), np.int32)
    leaving = np.zeros((n, n, chips.links), np.int32)
    for owner in range(n):
        image, root = moved(chips, owner)
        for tree in range(TREES):
            parent = [0] * n
            for chip in range(n):
                parent[image[chip]] = image[stored[root][tree][chip]]
            for chip in range(n):
                if chip == owner:
                    continue
                for link, other in chips.edges(parent[chip]):
                    if other == chip:
                        leaving[owner, parent[chip], link] = tree
                        parent_link[owner, chip, tree] = chips.back[link]
                        break
                at = chip
                while at != owner:
                    at = parent[at]
                    depth[owner, chip, tree] += 1
    return parent_link, depth, leaving


def flood(chips, rounds, parent_ref, leaving_ref, own_ref, land_ref, arrive, leave, send_sem, recv_sem):
    row, lmk = lax.axis_index("row"), lax.axis_index("lmk")
    steps = own_ref.shape[1]
    blocks = land_ref.shape[0]

    def each_link(act):
        for link in range(chips.links):
            here = chips.present(link, lmk)
            if here is None:
                act(link)
            else:
                pl.when(here)(functools.partial(act, link))

    def target(link):
        r, k = chips.neighbour(link, row, lmk)
        return {"row": r, "lmk": k}

    def outgoing(block, slot, link):
        return pltpu.make_async_remote_copy(
            src_ref=leave.at[block, slot, link],
            dst_ref=arrive.at[block, slot, chips.back[link]],
            send_sem=send_sem.at[block, slot, link],
            recv_sem=recv_sem.at[block, slot, chips.back[link]],
            device_id=target(link),
            device_id_type=MESH,
        )

    def incoming(block, slot, link):
        return pltpu.make_async_remote_copy(
            src_ref=leave.at[block, slot, link],
            dst_ref=arrive.at[block, slot, link],
            send_sem=send_sem.at[block, slot, link],
            recv_sem=recv_sem.at[block, slot, link],
            device_id=target(link),
            device_id_type=MESH,
        )

    barrier = pltpu.get_barrier_semaphore()

    def greet(link):
        pl.semaphore_signal(barrier, inc=1, device_id=target(link), device_id_type=MESH)

    each_link(greet)
    pl.semaphore_wait(barrier, chips.degree(lmk))

    def one_round(step, first, last):
        slot, before = step % 2, (step + 1) % 2
        for block in range(blocks):
            if not first:
                each_link(lambda link: incoming(block, before, link).wait_recv())
            held = []
            for tree in range(TREES):
                origin = parent_ref[block, tree]
                value = own_ref[tree, jnp.minimum(step, steps - 1)]
                if not first:
                    for link in range(chips.links):
                        value = lax.select(origin == link, arrive[block, before, link], value)
                land_ref[block, tree, step] = value
                held.append(value)
            if last:
                continue

            def send(link):
                if not first:

                    @pl.when(step >= 2)
                    def _():
                        outgoing(block, slot, link).wait_send()

                tree = leaving_ref[block, link]
                value = lax.select(tree == 1, held[1], held[0])
                leave[block, slot, link] = lax.select(tree == 2, held[2], value)
                outgoing(block, slot, link).start()

            each_link(send)

    one_round(0, True, False)

    def middle(step, carry):
        one_round(step, False, False)
        return carry

    lax.fori_loop(1, rounds - 1, middle, 0)
    one_round(rounds - 1, False, True)
    for block in range(blocks):
        for slot in range(2):
            each_link(lambda link: outgoing(block, slot, link).wait_send())


def normalize(widened):
    scale = lax.rsqrt(jnp.sum(widened * widened, axis=-1, keepdims=True) + 1e-06)
    return (widened * scale).astype(jnp.bfloat16)


def kernel_of(cosine, widths, weights):
    running = jnp.zeros(cosine.shape, jnp.float32)
    for which in range(widths.shape[0]):
        running = running + weights[which] * jnp.exp(2.0 * widths[which] * cosine)
    return running


def per_device(
    chips, embeddings, candidates, block_owner, landmark_picks, inverse_width, mixture, whitening
):
    me = lax.axis_index("row") * chips.lmks + lax.axis_index("lmk")
    core = lax.axis_index("bw")
    blocks, block_rows = landmark_picks.shape
    width = embeddings.shape[1]
    half = block_rows // 2
    steps = -(-half // (TREES * STEP_ROWS))
    parent_link, depth, leaving = routes(chips.rows, chips.lmks)
    deepest = int(depth.max())
    rounds = steps + deepest

    widths = lax.all_gather(inverse_width, "bw", tiled=True)
    weights = lax.all_gather(mixture, "bw", tiled=True)

    picks = jnp.where(block_owner[1] == me, landmark_picks[1], landmark_picks[0])
    picks = lax.dynamic_slice(picks, (core * half,), (half,))
    places = (picks[:, None] == jnp.arange(block_rows, dtype=jnp.int32)[None, :]).astype(jnp.bfloat16)
    chosen = normalize(jnp.dot(places, candidates, preferred_element_type=jnp.float32))
    own = jnp.pad(chosen, ((0, TREES * steps * STEP_ROWS - half), (0, 0)))
    own = own.reshape(TREES, steps, STEP_ROWS, width)

    my_parent = jnp.asarray(parent_link)[block_owner, me]
    my_depth = jnp.asarray(depth)[block_owner, me]
    my_leaving = jnp.asarray(leaving)[block_owner, me]

    slots = (blocks, 2, chips.links)
    landed = pl.pallas_call(
        functools.partial(flood, chips, rounds),
        out_shape=jax.ShapeDtypeStruct((blocks, TREES, rounds, STEP_ROWS, width), jnp.bfloat16),
        in_specs=[
            pl.BlockSpec(memory_space=pltpu.SMEM),
            pl.BlockSpec(memory_space=pltpu.SMEM),
            pl.BlockSpec(memory_space=pltpu.VMEM),
        ],
        out_specs=pl.BlockSpec(memory_space=pltpu.VMEM),
        scratch_shapes=[
            pltpu.VMEM(slots + (STEP_ROWS, width), jnp.bfloat16),
            pltpu.VMEM(slots + (STEP_ROWS, width), jnp.bfloat16),
            pltpu.SemaphoreType.DMA(slots),
            pltpu.SemaphoreType.DMA(slots),
        ],
        compiler_params=pltpu.CompilerParams(
            collective_id=0, has_side_effects=True, vmem_limit_bytes=32 * 1024 * 1024
        ),
        name="flood",
    )(my_parent, my_leaving, own)

    unit_rows = normalize(embeddings.astype(jnp.float32))
    parts = []
    for block in range(blocks):
        pieces = [
            lax.dynamic_slice(
                landed[block, tree], (my_depth[block, tree], 0, 0), (steps, STEP_ROWS, width)
            ).reshape(steps * STEP_ROWS, width)
            for tree in range(TREES)
        ]
        parts.append(jnp.concatenate(pieces)[:half])
    landmarks = jnp.concatenate(parts)
    cosine = jnp.einsum("rd,md->rm", unit_rows, landmarks, preferred_element_type=jnp.float32)
    mine = kernel_of(cosine, widths, weights).astype(jnp.bfloat16)
    other = lax.ppermute(mine, "bw", [(0, 1), (1, 0)])
    lower = jnp.where(core == 0, mine, other)
    upper = jnp.where(core == 0, other, mine)
    kernel = jnp.concatenate(
        [
            side[:, block * half : (block + 1) * half]
            for block in range(blocks)
            for side in (lower, upper)
        ],
        axis=1,
    )
    features = jnp.dot(kernel, whitening, preferred_element_type=jnp.float32)
    return features.astype(jnp.bfloat16)


def solution(mesh):
    chips = Chips(mesh.shape["row"], mesh.shape["lmk"])
    in_specs = (
        P(("row", "lmk"), None),
        P(("row", "lmk"), None),
        P(),
        P(),
        P("bw"),
        P("bw"),
        P(None, "bw"),
    )
    out_specs = P(("row", "lmk"), "bw")
    return jax.shard_map(
        functools.partial(per_device, chips),
        mesh=mesh,
        in_specs=in_specs,
        out_specs=out_specs,
        check_vma=False,
    )
```

```python
import functools
import math
import random

import jax
import jax.numpy as jnp
import numpy as np
from jax import lax
from jax.experimental import pallas as pl
from jax.experimental.pallas import tpu as pltpu
from jax.sharding import PartitionSpec as P

MESH = pl.DeviceIdType.MESH
TREES = 3
STEP_ROWS = 32


class Chips:
    def __init__(self, rows, lmks):
        self.rows, self.lmks = rows, lmks
        self.count = rows * lmks
        self.torus = rows != 4
        if self.torus:
            assert rows == 8 and lmks == 8
            self.back = (1, 0, 3, 2, 5, 4)
        else:
            self.back = (0, 1, 3, 2)
        self.links = len(self.back)

    def neighbour(self, link, row, lmk):
        if not self.torus:
            if link == 0:
                return (row + 2) % 4, lmk
            if link == 1:
                return row + 1 - 2 * (row % 2), lmk
            return row, lmk + (1 if link == 2 else -1)
        x, y, z = row % 4, lmk % 4, (row // 4) * 2 + lmk // 4
        step = 1 if link % 2 == 0 else 3
        if link // 2 == 0:
            x = (x + step) % 4
        elif link // 2 == 1:
            y = (y + step) % 4
        else:
            z = (z + step) % 4
        return (z // 2) * 4 + x, (z % 2) * 4 + y

    def present(self, link, lmk):
        if self.torus or link < 2:
            return None
        return lmk < self.lmks - 1 if link == 2 else lmk > 0

    def degree(self, lmk):
        if self.torus:
            return self.links
        return 2 + jnp.minimum(lmk, 1) + jnp.minimum(self.lmks - 1 - lmk, 1)

    def edges(self, chip):
        row, lmk = chip // self.lmks, chip % self.lmks
        for link in range(self.links):
            here = self.present(link, lmk)
            if here is None or here:
                r, k = self.neighbour(link, row, lmk)
                yield link, r * self.lmks + k


GRID_TREES = [
    [
        [0, 0, 1, 2, 5, 1, 2, 3, 9, 1, 2, 3, 13, 5, 13, 14],
        [0, 9, 10, 11, 12, 13, 14, 15, 0, 8, 9, 10, 8, 9, 10, 11],
        [0, 5, 6, 7, 0, 4, 5, 6, 12, 13, 14, 15, 4, 12, 6, 7],
    ],
    [
        [1, 1, 1, 2, 0, 4, 2, 3, 0, 10, 2, 3, 8, 14, 6, 7],
        [4, 1, 6, 7, 5, 1, 5, 6, 12, 13, 14, 15, 4, 5, 13, 14],
        [8, 1, 10, 11, 12, 13, 14, 15, 9, 1, 9, 10, 13, 9, 10, 11],
    ],
]


def torus_trees(chips):
    for seed in range(1000):
        draw = random.Random(seed)
        used, trees = set(), []
        for tree in range(TREES):
            parent, level = {0: 0}, [0]
            while level:
                following = []
                draw.shuffle(level)
                for chip in level:
                    for link, other in chips.edges(chip):
                        if other in parent or (chip, link) in used:
                            continue
                        if chip == 0 and link // 2 != tree:
                            continue
                        used.add((chip, link))
                        parent[other] = chip
                        following.append(other)
                level = following
            trees.append(parent)
        if all(len(parent) == chips.count for parent in trees):
            return [[parent[chip] for chip in range(chips.count)] for parent in trees]
    raise ValueError("no trees")


def moved(chips, owner):
    if not chips.torus:
        y, x, z = owner // 8, owner // 4 % 2, owner % 4
        turn = z >= 2
        image = [
            ((c // 8) ^ y) * 8 + ((c // 4 % 2) ^ x) * 4 + (3 - c % 4 if turn else c % 4)
            for c in range(16)
        ]
        return image, (3 - z if turn else z)

    def place(chip):
        row, lmk = chip // 8, chip % 8
        return row % 4, lmk % 4, (row // 4) * 2 + lmk // 4

    away = place(owner)
    image = []
    for chip in range(chips.count):
        x, y, z = ((a + b) % 4 for a, b in zip(place(chip), away))
        image.append(((z // 2) * 4 + x) * 8 + (z % 2) * 4 + y)
    return image, 0


@functools.lru_cache(maxsize=None)
def routes(rows, lmks):
    chips = Chips(rows, lmks)
    stored = [torus_trees(chips)] if chips.torus else GRID_TREES
    n = chips.count
    parent_link = np.full((n, n, TREES), -1, np.int32)
    depth = np.zeros((n, n, TREES), np.int32)
    leaving = np.zeros((n, n, chips.links), np.int32)
    for owner in range(n):
        image, root = moved(chips, owner)
        for tree in range(TREES):
            parent = [0] * n
            for chip in range(n):
                parent[image[chip]] = image[stored[root][tree][chip]]
            for chip in range(n):
                if chip == owner:
                    continue
                for link, other in chips.edges(parent[chip]):
                    if other == chip:
                        leaving[owner, parent[chip], link] = tree
                        parent_link[owner, chip, tree] = chips.back[link]
                        break
                at = chip
                while at != owner:
                    at = parent[at]
                    depth[owner, chip, tree] += 1
    return parent_link, depth, leaving


def fused(
    chips, rounds, deepest,
    owner_ref, table_ref, picks_ref, params_ref, rows_ref, candidates_ref, whitening_ref,
    features_ref,
    own, land, arrive, leave, columns, places, product, unit, fresh, cosine, mine, other, factor, total, held, theirs,
    send_sem, recv_sem, mine_sem, other_sem, params_sem, held_sem,
):
    row, lmk, core = lax.axis_index("row"), lax.axis_index("lmk"), lax.axis_index("bw")
    me = row * chips.lmks + lmk
    blocks = owner_ref.shape[0]
    block_rows, width = candidates_ref.shape
    half = block_rows // 2
    row_count, feature_count = total.shape
    span = TREES * STEP_ROWS
    steps = -(-half // span)
    partner = {"bw": 1 - core}

    def each_link(act):
        for link in range(chips.links):
            here = chips.present(link, lmk)
            if here is None:
                act(link)
            else:
                pl.when(here)(functools.partial(act, link))

    def target(link):
        r, k = chips.neighbour(link, row, lmk)
        return {"row": r, "lmk": k}

    def copy_to(link, block, slot, arriving):
        return pltpu.make_async_remote_copy(
            src_ref=leave.at[block, slot, link],
            dst_ref=arrive.at[block, slot, arriving],
            send_sem=send_sem.at[block, slot, link],
            recv_sem=recv_sem.at[block, slot, arriving],
            device_id=target(link),
            device_id_type=MESH,
        )

    def outgoing(block, slot, link):
        return copy_to(link, block, slot, chips.back[link])

    def incoming(block, slot, link):
        return copy_to(link, block, slot, link)

    def share(step):
        return pltpu.make_async_remote_copy(
            src_ref=mine.at[step],
            dst_ref=other.at[step + 1],
            send_sem=mine_sem.at[step],
            recv_sem=other_sem.at[step],
            device_id=partner,
            device_id_type=MESH,
        )

    params_copy = pltpu.make_async_remote_copy(
        src_ref=params_ref,
        dst_ref=theirs,
        send_sem=params_sem.at[0],
        recv_sem=params_sem.at[1],
        device_id=partner,
        device_id_type=MESH,
    )
    whole_rows = whitening_ref.shape[0]
    whitening_copy = pltpu.make_async_copy(whitening_ref, held.at[pl.ds(0, whole_rows)], held_sem)

    barrier = pltpu.get_barrier_semaphore()

    def greet(link):
        pl.semaphore_signal(barrier, inc=1, device_id=target(link), device_id_type=MESH)

    each_link(greet)
    pl.semaphore_signal(barrier, inc=1, device_id=partner, device_id_type=MESH)
    whitening_copy.start()

    first_word, second_word = [], []
    for block in range(blocks):
        at = 2 * (owner_ref[block] * chips.count + me)
        first_word.append(table_ref[at])
        second_word.append(table_ref[at + 1])

    def parent(block, tree):
        return (first_word[block] >> (3 * tree)) & 7

    def depth(block, tree):
        return (first_word[block] >> (9 + 4 * tree)) & 15

    def leaving(block, link):
        return (second_word[block] >> (2 * link)) & 3

    picked = lax.select(owner_ref[1] == me, picks_ref[1, core], picks_ref[0, core])
    for group in range(half // 128):
        columns[group * 128 : (group + 1) * 128] = jnp.transpose(
            jnp.broadcast_to(picked[group : group + 1], (128, 128))
        )
    columns[half:] = jnp.zeros_like(columns[half:])

    def normalize(widened):
        scale = lax.rsqrt(jnp.sum(widened * widened, axis=-1, keepdims=True) + 1e-06)
        return (widened * scale).astype(jnp.bfloat16)

    def gather(group):
        size = places.shape[0]
        lanes = lax.broadcasted_iota(jnp.int32, (size, 128), 1)
        wanted = columns[group * size : (group + 1) * size]
        for tile in range(block_rows // 128):
            places[:, tile * 128 : (tile + 1) * 128] = jnp.where(
                wanted == lanes + tile * 128, 1.0, 0.0
            ).astype(jnp.bfloat16)

        def tile_of(tile, carry):
            cols = pl.ds(pl.multiple_of(tile * 256, 256), 256)
            product[:, cols] = jnp.dot(
                places[...], candidates_ref[:, cols], preferred_element_type=jnp.float32
            )
            return carry

        lax.fori_loop(0, width // 256, tile_of, 0)

        def piece(index, carry):
            rows = pl.ds(pl.multiple_of(index * STEP_ROWS, STEP_ROWS), STEP_ROWS)
            own[group * (size // STEP_ROWS) + index] = normalize(product[rows])
            return carry

        lax.fori_loop(0, size // STEP_ROWS, piece, 0)

    groups = own.shape[0] * STEP_ROWS // places.shape[0]
    gather(0)
    pl.semaphore_wait(barrier, chips.degree(lmk) + 1)
    params_copy.start()

    def pass_on(step, first, last):
        slot, before = step % 2, (step + 1) % 2
        for block in range(blocks):
            if not first:
                each_link(lambda link: incoming(block, before, link).wait_recv())
            values = []
            for tree in range(TREES):
                origin = parent(block, tree)
                value = own[jnp.minimum(step, steps - 1) * TREES + tree]
                if not first:
                    for link in range(chips.links):
                        value = lax.select(origin == link + 1, arrive[block, before, link], value)
                land[block, tree, step] = value
                values.append(value)
            if last:
                continue

            def send(link):
                if not first:

                    @pl.when(step >= 2)
                    def _():
                        outgoing(block, slot, link).wait_send()

                tree = leaving(block, link)
                value = lax.select(tree == 1, values[1], values[0])
                leave[block, slot, link] = lax.select(tree == 2, values[2], value)
                outgoing(block, slot, link).start()

            each_link(send)

    def kernel_step(step):
        for block in range(blocks):
            for tree in range(TREES):
                fresh[pl.ds(block * span + tree * STEP_ROWS, STEP_ROWS)] = land[
                    block, tree, step + depth(block, tree)
                ]
        cosine[...] = lax.dot_general(
            unit[...], fresh[...], (((1,), (1,)), ((), ())), preferred_element_type=jnp.float32
        )
        spreads = params_ref.shape[0] // 2
        pairs = [
            [jnp.concatenate([ref[at : at + 1]] * (cosine.shape[1] // 128), axis=1) for at in (s, s + spreads)]
            for ref in (params_ref, theirs)
            for s in range(spreads)
        ]

        def strip(index, carry):
            rows = pl.ds(pl.multiple_of(index * 32, 32), 32)
            value = cosine[rows]
            running = jnp.zeros_like(value)
            for width_of, weight_of in pairs:
                running = running + weight_of * jnp.exp2(width_of * value)
            mine[step, rows] = running.astype(jnp.bfloat16)
            return carry

        lax.fori_loop(0, row_count // 32, strip, 0)
        share(step).start()

    def factor_rows(at, step, side):
        for block in range(blocks):
            for tree in range(TREES):
                start = block * block_rows + side * half + step * span + tree * STEP_ROWS
                value = held[pl.ds(pl.multiple_of(start, STEP_ROWS), STEP_ROWS)]
                if (steps - 1) * span + tree * STEP_ROWS >= half:
                    value = lax.select(step < steps - 1, value, jnp.zeros_like(value))
                to = at + block * span + tree * STEP_ROWS
                factor[to : to + STEP_ROWS] = value

    def feature_step(left):
        def tile_of(tile, carry):
            cols = pl.ds(pl.multiple_of(tile * 512, 512), 512)
            total[:, cols] += jnp.dot(
                left, factor[: left.shape[1], cols], preferred_element_type=jnp.float32
            )
            return carry

        lax.fori_loop(0, feature_count // 512, tile_of, 0)

    pass_on(0, True, False)
    for group in range(1, groups - 1):
        gather(group)

    def unit_piece(index, carry):
        rows = pl.ds(pl.multiple_of(index * 32, 32), 32)
        unit[rows] = normalize(rows_ref[rows].astype(jnp.float32))
        return carry

    pass_on(1, False, False)
    gather(groups - 1)
    pass_on(2, False, False)
    lax.fori_loop(0, row_count // 32, unit_piece, 0)
    fresh[...] = jnp.zeros_like(fresh)
    factor[...] = jnp.zeros_like(factor)
    total[...] = jnp.zeros_like(total)
    other[0] = jnp.zeros_like(other[0])
    params_copy.wait()

    def early(step, carry):
        pass_on(step, False, False)
        return carry

    lax.fori_loop(3, deepest, early, 0)
    whitening_copy.wait()
    padded = mine.shape[2]

    def work(step):
        kernel_step(step)

        @pl.when(step >= 1)
        def _():
            share(step - 1).wait_recv()

        factor_rows(0, step, core)
        factor_rows(padded, jnp.maximum(step - 1, 0), 1 - core)
        feature_step(jnp.concatenate([mine[step], other[step]], axis=1))

    def middle(step, carry):
        pass_on(step, False, False)
        work(step - deepest)
        return carry

    lax.fori_loop(deepest, rounds - 1, middle, 0)
    pass_on(rounds - 1, False, True)
    work(steps - 1)
    share(steps - 1).wait_recv()
    factor_rows(0, steps - 1, 1 - core)
    feature_step(other[steps])
    features_ref[...] = total[...].astype(jnp.bfloat16)

    for block in range(blocks):
        for slot in range(2):
            each_link(lambda link: outgoing(block, slot, link).wait_send())

    def sent(step, carry):
        share(step).wait_send()
        return carry

    lax.fori_loop(0, steps, sent, 0)


def per_device(
    chips, embeddings, candidates, block_owner, landmark_picks, inverse_width, mixture, whitening
):
    blocks, block_rows = landmark_picks.shape
    row_count, width = embeddings.shape
    feature_count = whitening.shape[1]
    half = block_rows // 2
    span = TREES * STEP_ROWS
    steps = -(-half // span)
    parent_link, depth, leaving = routes(chips.rows, chips.lmks)
    deepest = int(depth.max())
    rounds = steps + deepest
    padded = -(-blocks * span // 128) * 128
    group_rows = 4 * span
    own_rows = -(-half // group_rows) * group_rows

    first = sum((parent_link[..., t] + 1) << (3 * t) for t in range(TREES))
    first = first + sum(depth[..., t] << (9 + 4 * t) for t in range(TREES))
    second = sum(leaving[..., link] << (2 * link) for link in range(chips.links))
    table = np.stack([first, second], axis=-1).reshape(-1).astype(np.int32)

    params = jnp.concatenate([inverse_width * (2.0 * math.log2(math.e)), mixture])
    params = jnp.broadcast_to(params[:, None], (params.shape[0], 128))
    picks = landmark_picks.reshape(blocks, 2, half // 128, 128)

    slots = (blocks, 2, chips.links)
    bf16, f32 = jnp.bfloat16, jnp.float32
    in_vmem = pl.BlockSpec(memory_space=pltpu.VMEM)
    in_smem = pl.BlockSpec(memory_space=pltpu.SMEM)
    return pl.pallas_call(
        functools.partial(fused, chips, rounds, deepest),
        out_shape=jax.ShapeDtypeStruct((row_count, feature_count), bf16),
        in_specs=[in_smem, in_smem] + [in_vmem] * 4 + [pl.BlockSpec(memory_space=pl.ANY)],
        out_specs=in_vmem,
        scratch_shapes=[
            pltpu.VMEM((own_rows // STEP_ROWS, STEP_ROWS, width), bf16),
            pltpu.VMEM((blocks, TREES, rounds, STEP_ROWS, width), bf16),
            pltpu.VMEM(slots + (STEP_ROWS, width), bf16),
            pltpu.VMEM(slots + (STEP_ROWS, width), bf16),
            pltpu.VMEM((own_rows, 128), jnp.int32),
            pltpu.VMEM((group_rows, block_rows), bf16),
            pltpu.VMEM((group_rows, width), f32),
            pltpu.VMEM((row_count, width), bf16),
            pltpu.VMEM((padded, width), bf16),
            pltpu.VMEM((row_count, padded), f32),
            pltpu.VMEM((steps, row_count, padded), bf16),
            pltpu.VMEM((steps + 1, row_count, padded), bf16),
            pltpu.VMEM((2 * padded, feature_count), bf16),
            pltpu.VMEM((row_count, feature_count), f32),
            pltpu.VMEM((whitening.shape[0] + STEP_ROWS, feature_count), bf16),
            pltpu.VMEM(params.shape, f32),
            pltpu.SemaphoreType.DMA(slots),
            pltpu.SemaphoreType.DMA(slots),
            pltpu.SemaphoreType.DMA((steps,)),
            pltpu.SemaphoreType.DMA((steps,)),
            pltpu.SemaphoreType.DMA((2,)),
            pltpu.SemaphoreType.DMA,
        ],
        compiler_params=pltpu.CompilerParams(
            collective_id=0, has_side_effects=True, vmem_limit_bytes=60 * 1024 * 1024
        ),
        name="fused",
    )(block_owner, jnp.asarray(table), picks, params, embeddings, candidates, whitening)


def solution(mesh):
    chips = Chips(mesh.shape["row"], mesh.shape["lmk"])
    in_specs = (
        P(("row", "lmk"), None),
        P(("row", "lmk"), None),
        P(),
        P(),
        P("bw"),
        P("bw"),
        P(None, "bw"),
    )
    out_specs = P(("row", "lmk"), "bw")
    return jax.shard_map(
        functools.partial(per_device, chips),
        mesh=mesh,
        in_specs=in_specs,
        out_specs=out_specs,
        check_vma=False,
    )
```

```python
import functools
import math
import random

import jax
import jax.numpy as jnp
import numpy as np
from jax import lax
from jax.experimental import pallas as pl
from jax.experimental.pallas import tpu as pltpu
from jax.sharding import PartitionSpec as P

MESH = pl.DeviceIdType.MESH
TREES = 3
STEP_ROWS = 32


class Chips:
    def __init__(self, rows, lmks):
        self.rows, self.lmks = rows, lmks
        self.count = rows * lmks
        self.torus = rows != 4
        if self.torus:
            assert rows == 8 and lmks == 8
            self.back = (1, 0, 3, 2, 5, 4)
        else:
            self.back = (0, 1, 3, 2)
        self.links = len(self.back)

    def neighbour(self, link, row, lmk):
        if not self.torus:
            if link == 0:
                return (row + 2) % 4, lmk
            if link == 1:
                return row + 1 - 2 * (row % 2), lmk
            return row, lmk + (1 if link == 2 else -1)
        x, y, z = row % 4, lmk % 4, (row // 4) * 2 + lmk // 4
        step = 1 if link % 2 == 0 else 3
        if link // 2 == 0:
            x = (x + step) % 4
        elif link // 2 == 1:
            y = (y + step) % 4
        else:
            z = (z + step) % 4
        return (z // 2) * 4 + x, (z % 2) * 4 + y

    def present(self, link, lmk):
        if self.torus or link < 2:
            return None
        return lmk < self.lmks - 1 if link == 2 else lmk > 0

    def degree(self, lmk):
        if self.torus:
            return self.links
        return 2 + jnp.minimum(lmk, 1) + jnp.minimum(self.lmks - 1 - lmk, 1)

    def edges(self, chip):
        row, lmk = chip // self.lmks, chip % self.lmks
        for link in range(self.links):
            here = self.present(link, lmk)
            if here is None or here:
                r, k = self.neighbour(link, row, lmk)
                yield link, r * self.lmks + k


GRID_TREES = [
    [
        [0, 0, 1, 2, 5, 1, 2, 3, 9, 1, 2, 3, 13, 5, 13, 14],
        [0, 9, 10, 11, 12, 13, 14, 15, 0, 8, 9, 10, 8, 9, 10, 11],
        [0, 5, 6, 7, 0, 4, 5, 6, 12, 13, 14, 15, 4, 12, 6, 7],
    ],
    [
        [1, 1, 1, 2, 0, 4, 2, 3, 0, 10, 2, 3, 8, 14, 6, 7],
        [4, 1, 6, 7, 5, 1, 5, 6, 12, 13, 14, 15, 4, 5, 13, 14],
        [8, 1, 10, 11, 12, 13, 14, 15, 9, 1, 9, 10, 13, 9, 10, 11],
    ],
]


def torus_trees(chips):
    for seed in range(1000):
        draw = random.Random(seed)
        used, trees = set(), []
        for tree in range(TREES):
            parent, level = {0: 0}, [0]
            while level:
                following = []
                draw.shuffle(level)
                for chip in level:
                    for link, other in chips.edges(chip):
                        if other in parent or (chip, link) in used:
                            continue
                        if chip == 0 and link // 2 != tree:
                            continue
                        used.add((chip, link))
                        parent[other] = chip
                        following.append(other)
                level = following
            trees.append(parent)
        if all(len(parent) == chips.count for parent in trees):
            return [[parent[chip] for chip in range(chips.count)] for parent in trees]
    raise ValueError("no trees")


def moved(chips, owner):
    if not chips.torus:
        y, x, z = owner // 8, owner // 4 % 2, owner % 4
        turn = z >= 2
        image = [
            ((c // 8) ^ y) * 8 + ((c // 4 % 2) ^ x) * 4 + (3 - c % 4 if turn else c % 4)
            for c in range(16)
        ]
        return image, (3 - z if turn else z)

    def place(chip):
        row, lmk = chip // 8, chip % 8
        return row % 4, lmk % 4, (row // 4) * 2 + lmk // 4

    away = place(owner)
    image = []
    for chip in range(chips.count):
        x, y, z = ((a + b) % 4 for a, b in zip(place(chip), away))
        image.append(((z // 2) * 4 + x) * 8 + (z % 2) * 4 + y)
    return image, 0


@functools.lru_cache(maxsize=None)
def routes(rows, lmks):
    chips = Chips(rows, lmks)
    stored = [torus_trees(chips)] if chips.torus else GRID_TREES
    n = chips.count
    parent_link = np.full((n, n, TREES), -1, np.int32)
    depth = np.zeros((n, n, TREES), np.int32)
    leaving = np.zeros((n, n, chips.links), np.int32)
    for owner in range(n):
        image, root = moved(chips, owner)
        for tree in range(TREES):
            parent = [0] * n
            for chip in range(n):
                parent[image[chip]] = image[stored[root][tree][chip]]
            for chip in range(n):
                if chip == owner:
                    continue
                for link, other in chips.edges(parent[chip]):
                    if other == chip:
                        leaving[owner, parent[chip], link] = tree
                        parent_link[owner, chip, tree] = chips.back[link]
                        break
                at = chip
                while at != owner:
                    at = parent[at]
                    depth[owner, chip, tree] += 1
    return parent_link, depth, leaving


def fused(
    chips, rounds, deepest,
    owner_ref, table_ref, widths_ref, weights_ref, picks_ref, rows_ref, candidates_ref, whitening_ref,
    features_ref,
    own, land, arrive, leave, columns, places, product, unit, fresh, cosine, mine, other, factor, total, held, params_ref, theirs,
    send_sem, recv_sem, mine_sem, other_sem, params_sem, held_sem,
):
    row, lmk, core = lax.axis_index("row"), lax.axis_index("lmk"), lax.axis_index("bw")
    me = row * chips.lmks + lmk
    blocks = owner_ref.shape[0]
    block_rows, width = candidates_ref.shape
    half = block_rows // 2
    row_count, feature_count = total.shape
    span = TREES * STEP_ROWS
    steps = -(-half // span)
    partner = {"bw": 1 - core}

    def each_link(act):
        for link in range(chips.links):
            here = chips.present(link, lmk)
            if here is None:
                act(link)
            else:
                pl.when(here)(functools.partial(act, link))

    def target(link):
        r, k = chips.neighbour(link, row, lmk)
        return {"row": r, "lmk": k}

    def copy_to(link, block, slot, arriving):
        return pltpu.make_async_remote_copy(
            src_ref=leave.at[block, slot, link],
            dst_ref=arrive.at[block, slot, arriving],
            send_sem=send_sem.at[block, slot, link],
            recv_sem=recv_sem.at[block, slot, arriving],
            device_id=target(link),
            device_id_type=MESH,
        )

    def outgoing(block, slot, link):
        return copy_to(link, block, slot, chips.back[link])

    def incoming(block, slot, link):
        return copy_to(link, block, slot, link)

    def share(step):
        return pltpu.make_async_remote_copy(
            src_ref=mine.at[step],
            dst_ref=other.at[step + 1],
            send_sem=mine_sem.at[step],
            recv_sem=other_sem.at[step],
            device_id=partner,
            device_id_type=MESH,
        )

    params_copy = pltpu.make_async_remote_copy(
        src_ref=params_ref,
        dst_ref=theirs,
        send_sem=params_sem.at[0],
        recv_sem=params_sem.at[1],
        device_id=partner,
        device_id_type=MESH,
    )
    whole_rows = whitening_ref.shape[0]
    whitening_copy = pltpu.make_async_copy(whitening_ref, held.at[pl.ds(0, whole_rows)], held_sem)

    barrier = pltpu.get_barrier_semaphore()

    def greet(link):
        pl.semaphore_signal(barrier, inc=1, device_id=target(link), device_id_type=MESH)

    each_link(greet)
    pl.semaphore_signal(barrier, inc=1, device_id=partner, device_id_type=MESH)
    whitening_copy.start()

    first_word, second_word = [], []
    for block in range(blocks):
        at = 2 * (owner_ref[block] * chips.count + me)
        first_word.append(table_ref[at])
        second_word.append(table_ref[at + 1])

    def parent(block, tree):
        return (first_word[block] >> (3 * tree)) & 7

    def depth(block, tree):
        return (first_word[block] >> (9 + 4 * tree)) & 15

    def leaving(block, link):
        return (second_word[block] >> (2 * link)) & 3

    for group in range(half // 128):
        lanes_of = pl.ds(pl.multiple_of(core * half + group * 128, 128), 128)
        picked = lax.select(owner_ref[1] == me, picks_ref[1:2, lanes_of], picks_ref[0:1, lanes_of])
        columns[group * 128 : (group + 1) * 128] = jnp.transpose(jnp.broadcast_to(picked, (128, 128)))
    columns[half:] = jnp.zeros_like(columns[half:])

    def normalize(widened):
        scale = lax.rsqrt(jnp.sum(widened * widened, axis=-1, keepdims=True) + 1e-06)
        return (widened * scale).astype(jnp.bfloat16)

    def gather(group):
        size = places.shape[0]
        lanes = lax.broadcasted_iota(jnp.int32, (size, 128), 1)
        wanted = columns[group * size : (group + 1) * size]
        for tile in range(block_rows // 128):
            places[:, tile * 128 : (tile + 1) * 128] = jnp.where(
                wanted == lanes + tile * 128, 1.0, 0.0
            ).astype(jnp.bfloat16)

        def tile_of(tile, carry):
            cols = pl.ds(pl.multiple_of(tile * 256, 256), 256)
            product[:, cols] = jnp.dot(
                places[...], candidates_ref[:, cols], preferred_element_type=jnp.float32
            )
            return carry

        lax.fori_loop(0, width // 256, tile_of, 0)

        def piece(index, carry):
            rows = pl.ds(pl.multiple_of(index * STEP_ROWS, STEP_ROWS), STEP_ROWS)
            own[group * (size // STEP_ROWS) + index] = normalize(product[rows])
            return carry

        lax.fori_loop(0, size // STEP_ROWS, piece, 0)

    spreads = widths_ref.shape[0]
    for s in range(spreads):
        params_ref[s : s + 1] = jnp.full((1, 128), widths_ref[s] * (2.0 * math.log2(math.e)), jnp.float32)
        params_ref[spreads + s : spreads + s + 1] = jnp.full((1, 128), weights_ref[s], jnp.float32)

    groups = own.shape[0] * STEP_ROWS // places.shape[0]
    gather(0)
    pl.semaphore_wait(barrier, chips.degree(lmk) + 1)
    params_copy.start()

    def pass_on(block, step, first=False, last=False):
        slot, before = step % 2, (step + 1) % 2
        if not first:
            each_link(lambda link: incoming(block, before, link).wait_recv())
        values = []
        for tree in range(TREES):
            origin = parent(block, tree)
            value = own[jnp.minimum(step, steps - 1) * TREES + tree]
            if not first:
                for link in range(chips.links):
                    value = lax.select(origin == link + 1, arrive[block, before, link], value)
            land[block, tree, step] = value
            values.append(value)
        if last:
            return

        def send(link):
            if not first:

                @pl.when(step >= 2)
                def _():
                    outgoing(block, slot, link).wait_send()

            tree = leaving(block, link)
            value = lax.select(tree == 1, values[1], values[0])
            leave[block, slot, link] = lax.select(tree == 2, values[2], value)
            outgoing(block, slot, link).start()

        each_link(send)

    def kernel_step(step):
        for block in range(blocks):
            for tree in range(TREES):
                fresh[pl.ds(block * span + tree * STEP_ROWS, STEP_ROWS)] = land[
                    block, tree, step + depth(block, tree)
                ]
        cosine[...] = lax.dot_general(
            unit[...], fresh[...], (((1,), (1,)), ((), ())), preferred_element_type=jnp.float32
        )
        pairs = [
            [jnp.concatenate([ref[at : at + 1]] * (cosine.shape[1] // 128), axis=1) for at in (s, s + spreads)]
            for ref in (params_ref, theirs)
            for s in range(spreads)
        ]

        def strip(index, carry):
            rows = pl.ds(pl.multiple_of(index * 32, 32), 32)
            value = cosine[rows]
            running = jnp.zeros_like(value)
            for width_of, weight_of in pairs:
                running = running + weight_of * jnp.exp2(width_of * value)
            mine[step, rows] = running.astype(jnp.bfloat16)
            return carry

        lax.fori_loop(0, row_count // 32, strip, 0)
        share(step).start()

    def factor_rows(at, step, side):
        for block in range(blocks):
            for tree in range(TREES):
                start = block * block_rows + side * half + step * span + tree * STEP_ROWS
                value = held[pl.ds(pl.multiple_of(start, STEP_ROWS), STEP_ROWS)]
                if (steps - 1) * span + tree * STEP_ROWS >= half:
                    value = lax.select(step < steps - 1, value, jnp.zeros_like(value))
                to = at + block * span + tree * STEP_ROWS
                factor[to : to + STEP_ROWS] = value

    def feature_step(left):
        def tile_of(tile, carry):
            cols = pl.ds(pl.multiple_of(tile * 512, 512), 512)
            total[:, cols] += jnp.dot(
                left, factor[: left.shape[1], cols], preferred_element_type=jnp.float32
            )
            return carry

        lax.fori_loop(0, feature_count // 512, tile_of, 0)

    def unit_piece(index, carry):
        rows = pl.ds(pl.multiple_of(index * 32, 32), 32)
        unit[rows] = normalize(rows_ref[rows].astype(jnp.float32))
        return carry

    pass_on(0, 0, first=True)
    pass_on(1, 0, first=True)
    for group in range(1, groups - 1):
        gather(group)
    pass_on(0, 1)
    gather(groups - 1)
    pass_on(1, 1)
    pass_on(0, 2)
    lax.fori_loop(0, row_count // 32, unit_piece, 0)
    fresh[...] = jnp.zeros_like(fresh)
    pass_on(1, 2)
    factor[...] = jnp.zeros_like(factor)
    total[...] = jnp.zeros_like(total)
    other[0] = jnp.zeros_like(other[0])
    params_copy.wait()

    def early(step, carry):
        pass_on(0, step)
        pass_on(1, step)
        return carry

    lax.fori_loop(3, deepest, early, 0)
    whitening_copy.wait()
    padded = mine.shape[2]

    def features_of(step):
        @pl.when(step >= 1)
        def _():
            share(step - 1).wait_recv()

        factor_rows(0, step, core)
        factor_rows(padded, jnp.maximum(step - 1, 0), 1 - core)
        feature_step(jnp.concatenate([mine[step], other[step]], axis=1))

    pass_on(0, deepest)
    pass_on(1, deepest)
    kernel_step(0)

    def middle(step, carry):
        pass_on(0, step)
        features_of(step - deepest - 1)
        pass_on(1, step)
        kernel_step(step - deepest)
        return carry

    lax.fori_loop(deepest + 1, rounds - 1, middle, 0)
    pass_on(0, rounds - 1, last=True)
    features_of(steps - 2)
    pass_on(1, rounds - 1, last=True)
    kernel_step(steps - 1)
    features_of(steps - 1)
    share(steps - 1).wait_recv()
    factor_rows(0, steps - 1, 1 - core)
    feature_step(other[steps])
    features_ref[...] = total[...].astype(jnp.bfloat16)

    for block in range(blocks):
        for slot in range(2):
            each_link(lambda link: outgoing(block, slot, link).wait_send())

    def sent(step, carry):
        share(step).wait_send()
        return carry

    lax.fori_loop(0, steps, sent, 0)


def per_device(
    chips, embeddings, candidates, block_owner, landmark_picks, inverse_width, mixture, whitening
):
    blocks, block_rows = landmark_picks.shape
    row_count, width = embeddings.shape
    feature_count = whitening.shape[1]
    half = block_rows // 2
    span = TREES * STEP_ROWS
    steps = -(-half // span)
    parent_link, depth, leaving = routes(chips.rows, chips.lmks)
    deepest = int(depth.max())
    rounds = steps + deepest
    padded = -(-blocks * span // 128) * 128
    group_rows = 4 * span
    own_rows = -(-half // group_rows) * group_rows

    first = sum((parent_link[..., t] + 1) << (3 * t) for t in range(TREES))
    first = first + sum(depth[..., t] << (9 + 4 * t) for t in range(TREES))
    second = sum(leaving[..., link] << (2 * link) for link in range(chips.links))
    table = np.stack([first, second], axis=-1).reshape(-1).astype(np.int32)

    slots = (blocks, 2, chips.links)
    bf16, f32 = jnp.bfloat16, jnp.float32
    in_vmem = pl.BlockSpec(memory_space=pltpu.VMEM)
    in_smem = pl.BlockSpec(memory_space=pltpu.SMEM)
    return pl.pallas_call(
        functools.partial(fused, chips, rounds, deepest),
        out_shape=jax.ShapeDtypeStruct((row_count, feature_count), bf16),
        in_specs=[in_smem] * 4 + [in_vmem] * 3 + [pl.BlockSpec(memory_space=pl.ANY)],
        out_specs=in_vmem,
        scratch_shapes=[
            pltpu.VMEM((own_rows // STEP_ROWS, STEP_ROWS, width), bf16),
            pltpu.VMEM((blocks, TREES, rounds, STEP_ROWS, width), bf16),
            pltpu.VMEM(slots + (STEP_ROWS, width), bf16),
            pltpu.VMEM(slots + (STEP_ROWS, width), bf16),
            pltpu.VMEM((own_rows, 128), jnp.int32),
            pltpu.VMEM((group_rows, block_rows), bf16),
            pltpu.VMEM((group_rows, width), f32),
            pltpu.VMEM((row_count, width), bf16),
            pltpu.VMEM((padded, width), bf16),
            pltpu.VMEM((row_count, padded), f32),
            pltpu.VMEM((steps, row_count, padded), bf16),
            pltpu.VMEM((steps + 1, row_count, padded), bf16),
            pltpu.VMEM((2 * padded, feature_count), bf16),
            pltpu.VMEM((row_count, feature_count), f32),
            pltpu.VMEM((whitening.shape[0] + STEP_ROWS, feature_count), bf16),
            pltpu.VMEM((2 * inverse_width.shape[0], 128), f32),
            pltpu.VMEM((2 * inverse_width.shape[0], 128), f32),
            pltpu.SemaphoreType.DMA(slots),
            pltpu.SemaphoreType.DMA(slots),
            pltpu.SemaphoreType.DMA((steps,)),
            pltpu.SemaphoreType.DMA((steps,)),
            pltpu.SemaphoreType.DMA((2,)),
            pltpu.SemaphoreType.DMA,
        ],
        compiler_params=pltpu.CompilerParams(
            collective_id=0, has_side_effects=True, vmem_limit_bytes=60 * 1024 * 1024
        ),
        name="fused",
    )(block_owner, jnp.asarray(table), inverse_width, mixture, landmark_picks, embeddings, candidates, whitening)


def solution(mesh):
    chips = Chips(mesh.shape["row"], mesh.shape["lmk"])
    in_specs = (
        P(("row", "lmk"), None),
        P(("row", "lmk"), None),
        P(),
        P(),
        P("bw"),
        P("bw"),
        P(None, "bw"),
    )
    out_specs = P(("row", "lmk"), "bw")
    return jax.shard_map(
        functools.partial(per_device, chips),
        mesh=mesh,
        in_specs=in_specs,
        out_specs=out_specs,
        check_vma=False,
    )
```

```python
import functools
import math
import random

import jax
import jax.numpy as jnp
import numpy as np
from jax import lax
from jax.experimental import pallas as pl
from jax.experimental.pallas import tpu as pltpu
from jax.sharding import PartitionSpec as P

MESH = pl.DeviceIdType.MESH
TREES = 3
STEP_ROWS = 16
LAG = 2
BATCH = 4


class Chips:
    def __init__(self, rows, lmks):
        self.rows, self.lmks = rows, lmks
        self.count = rows * lmks
        self.torus = rows != 4
        if self.torus:
            assert rows == 8 and lmks == 8
            self.back = (1, 0, 3, 2, 5, 4)
        else:
            self.back = (0, 1, 3, 2)
        self.links = len(self.back)

    def neighbour(self, link, row, lmk):
        if not self.torus:
            if link == 0:
                return (row + 2) % 4, lmk
            if link == 1:
                return row + 1 - 2 * (row % 2), lmk
            return row, lmk + (1 if link == 2 else -1)
        x, y, z = row % 4, lmk % 4, (row // 4) * 2 + lmk // 4
        step = 1 if link % 2 == 0 else 3
        if link // 2 == 0:
            x = (x + step) % 4
        elif link // 2 == 1:
            y = (y + step) % 4
        else:
            z = (z + step) % 4
        return (z // 2) * 4 + x, (z % 2) * 4 + y

    def present(self, link, lmk):
        if self.torus or link < 2:
            return None
        return lmk < self.lmks - 1 if link == 2 else lmk > 0

    def degree(self, lmk):
        if self.torus:
            return self.links
        return 2 + jnp.minimum(lmk, 1) + jnp.minimum(self.lmks - 1 - lmk, 1)

    def edges(self, chip):
        row, lmk = chip // self.lmks, chip % self.lmks
        for link in range(self.links):
            here = self.present(link, lmk)
            if here is None or here:
                r, k = self.neighbour(link, row, lmk)
                yield link, r * self.lmks + k


GRID_TREES = [
    [
        [0, 0, 1, 2, 5, 1, 2, 3, 9, 1, 2, 3, 13, 5, 13, 14],
        [0, 9, 10, 11, 12, 13, 14, 15, 0, 8, 9, 10, 8, 9, 10, 11],
        [0, 5, 6, 7, 0, 4, 5, 6, 12, 13, 14, 15, 4, 12, 6, 7],
    ],
    [
        [1, 1, 1, 2, 0, 4, 2, 3, 0, 10, 2, 3, 8, 14, 6, 7],
        [4, 1, 6, 7, 5, 1, 5, 6, 12, 13, 14, 15, 4, 5, 13, 14],
        [8, 1, 10, 11, 12, 13, 14, 15, 9, 1, 9, 10, 13, 9, 10, 11],
    ],
]


def torus_trees(chips):
    for seed in range(1000):
        draw = random.Random(seed)
        used, trees = set(), []
        for tree in range(TREES):
            parent, level = {0: 0}, [0]
            while level:
                following = []
                draw.shuffle(level)
                for chip in level:
                    for link, other in chips.edges(chip):
                        if other in parent or (chip, link) in used:
                            continue
                        if chip == 0 and link // 2 != tree:
                            continue
                        used.add((chip, link))
                        parent[other] = chip
                        following.append(other)
                level = following
            trees.append(parent)
        if all(len(parent) == chips.count for parent in trees):
            return [[parent[chip] for chip in range(chips.count)] for parent in trees]
    raise ValueError("no trees")


def moved(chips, owner):
    if not chips.torus:
        y, x, z = owner // 8, owner // 4 % 2, owner % 4
        turn = z >= 2
        image = [
            ((c // 8) ^ y) * 8 + ((c // 4 % 2) ^ x) * 4 + (3 - c % 4 if turn else c % 4)
            for c in range(16)
        ]
        return image, (3 - z if turn else z)

    def place(chip):
        row, lmk = chip // 8, chip % 8
        return row % 4, lmk % 4, (row // 4) * 2 + lmk // 4

    away = place(owner)
    image = []
    for chip in range(chips.count):
        x, y, z = ((a + b) % 4 for a, b in zip(place(chip), away))
        image.append(((z // 2) * 4 + x) * 8 + (z % 2) * 4 + y)
    return image, 0


@functools.lru_cache(maxsize=None)
def routes(rows, lmks):
    chips = Chips(rows, lmks)
    stored = [torus_trees(chips)] if chips.torus else GRID_TREES
    n = chips.count
    parent_link = np.full((n, n, TREES), -1, np.int32)
    depth = np.zeros((n, n, TREES), np.int32)
    leaving = np.zeros((n, n, chips.links), np.int32)
    for owner in range(n):
        image, root = moved(chips, owner)
        for tree in range(TREES):
            parent = [0] * n
            for chip in range(n):
                parent[image[chip]] = image[stored[root][tree][chip]]
            for chip in range(n):
                if chip == owner:
                    continue
                for link, other in chips.edges(parent[chip]):
                    if other == chip:
                        leaving[owner, parent[chip], link] = tree
                        parent_link[owner, chip, tree] = chips.back[link]
                        break
                at = chip
                while at != owner:
                    at = parent[at]
                    depth[owner, chip, tree] += 1
    return parent_link, depth, leaving


def fused(
    chips, rounds, deepest,
    owner_ref, table_ref, widths_ref, weights_ref, picks_ref, rows_ref, candidates_ref, whitening_ref,
    features_ref,
    own, land, arrive, leave, columns, places, product, unit, fresh, cosine, mine, other, mine_last, other_last, factor, total, held, params_ref, theirs,
    send_sem, recv_sem, mine_sem, other_sem, last_sem, params_sem, held_sem,
):
    row, lmk, core = lax.axis_index("row"), lax.axis_index("lmk"), lax.axis_index("bw")
    me = row * chips.lmks + lmk
    blocks = owner_ref.shape[0]
    block_rows, width = candidates_ref.shape
    half = block_rows // 2
    row_count, feature_count = total.shape
    span = TREES * STEP_ROWS
    steps = -(-half // span)
    partner = {"bw": 1 - core}

    def each_link(act):
        for link in range(chips.links):
            here = chips.present(link, lmk)
            if here is None:
                act(link)
            else:
                pl.when(here)(functools.partial(act, link))

    def target(link):
        r, k = chips.neighbour(link, row, lmk)
        return {"row": r, "lmk": k}

    def copy_to(link, block, slot, arriving):
        return pltpu.make_async_remote_copy(
            src_ref=leave.at[block, slot, link],
            dst_ref=arrive.at[block, slot, arriving],
            send_sem=send_sem.at[block, slot, link],
            recv_sem=recv_sem.at[block, slot, arriving],
            device_id=target(link),
            device_id_type=MESH,
        )

    def outgoing(block, slot, link):
        return copy_to(link, block, slot, chips.back[link])

    def incoming(block, slot, link):
        return copy_to(link, block, slot, link)

    def share(step):
        return pltpu.make_async_remote_copy(
            src_ref=mine.at[step],
            dst_ref=other.at[step + 1],
            send_sem=mine_sem.at[step],
            recv_sem=other_sem.at[step],
            device_id=partner,
            device_id_type=MESH,
        )

    share_last = pltpu.make_async_remote_copy(
        src_ref=mine_last,
        dst_ref=other_last,
        send_sem=last_sem.at[0],
        recv_sem=last_sem.at[1],
        device_id=partner,
        device_id_type=MESH,
    )
    params_copy = pltpu.make_async_remote_copy(
        src_ref=params_ref,
        dst_ref=theirs,
        send_sem=params_sem.at[0],
        recv_sem=params_sem.at[1],
        device_id=partner,
        device_id_type=MESH,
    )
    whitening_copy = pltpu.make_async_copy(whitening_ref, held, held_sem)

    barrier = pltpu.get_barrier_semaphore()

    def greet(link):
        pl.semaphore_signal(barrier, inc=1, device_id=target(link), device_id_type=MESH)

    each_link(greet)
    pl.semaphore_signal(barrier, inc=1, device_id=partner, device_id_type=MESH)
    whitening_copy.start()

    first_word, second_word = [], []
    for block in range(blocks):
        at = 2 * (owner_ref[block] * chips.count + me)
        first_word.append(table_ref[at])
        second_word.append(table_ref[at + 1])

    def parent(block, tree):
        return (first_word[block] >> (3 * tree)) & 7

    def depth(block, tree):
        return (first_word[block] >> (9 + 4 * tree)) & 15

    def leaving(block, link):
        return (second_word[block] >> (2 * link)) & 3

    for group in range(half // 128):
        lanes_of = pl.ds(pl.multiple_of(core * half + group * 128, 128), 128)
        picked = lax.select(owner_ref[1] == me, picks_ref[1:2, lanes_of], picks_ref[0:1, lanes_of])
        columns[group * 128 : (group + 1) * 128] = jnp.transpose(jnp.broadcast_to(picked, (128, 128)))
    columns[half:] = jnp.zeros_like(columns[half:])

    def normalize(widened):
        scale = lax.rsqrt(jnp.sum(widened * widened, axis=-1, keepdims=True) + 1e-06)
        return (widened * scale).astype(jnp.bfloat16)

    def products(first_tile, last_tile):
        def tile_of(tile, carry):
            cols = pl.ds(pl.multiple_of(tile * 256, 256), 256)
            product[:, cols] = jnp.dot(
                places[...], candidates_ref[:, cols], preferred_element_type=jnp.float32
            )
            return carry

        lax.fori_loop(first_tile, last_tile, tile_of, 0)

    tiles = width // 256

    def gather_start(group):
        size = places.shape[0]
        lanes = lax.broadcasted_iota(jnp.int32, (size, 128), 1)
        wanted = columns[group * size : (group + 1) * size]
        for tile in range(block_rows // 128):
            places[:, tile * 128 : (tile + 1) * 128] = jnp.where(
                wanted == lanes + tile * 128, 1.0, 0.0
            ).astype(jnp.bfloat16)
        products(0, tiles // 2)

    def gather_end(group):
        products(tiles // 2, tiles)
        pieces = places.shape[0] // STEP_ROWS

        def piece(index, carry):
            rows = pl.ds(pl.multiple_of(index * STEP_ROWS, STEP_ROWS), STEP_ROWS)
            own[group * pieces + index] = normalize(product[rows])
            return carry

        lax.fori_loop(0, pieces, piece, 0)

    spreads = widths_ref.shape[0]
    for s in range(spreads):
        params_ref[s : s + 1] = jnp.full((1, 128), widths_ref[s] * (2.0 * math.log2(math.e)), jnp.float32)
        params_ref[spreads + s : spreads + s + 1] = jnp.full((1, 128), weights_ref[s], jnp.float32)

    groups = own.shape[0] * STEP_ROWS // places.shape[0]
    gather_start(0)
    gather_end(0)
    pl.semaphore_wait(barrier, chips.degree(lmk) + 1)
    params_copy.start()

    def pass_on(block, step, first=False, last=False):
        slot, before = step % (2 * LAG), (step + LAG) % (2 * LAG)
        if not first:
            each_link(lambda link: incoming(block, before, link).wait_recv())
        values = []
        for tree in range(TREES):
            origin = parent(block, tree)
            value = own[jnp.minimum(step, steps - 1) * TREES + tree]
            if not first:
                for link in range(chips.links):
                    value = lax.select(origin == link + 1, arrive[block, before, link], value)
            land[block, tree, step] = value
            values.append(value)
        if last:
            return

        def send(link):
            if not first:

                @pl.when(step >= 2 * LAG)
                def _():
                    outgoing(block, slot, link).wait_send()

            tree = leaving(block, link)
            value = lax.select(tree == 1, values[1], values[0])
            leave[block, slot, link] = lax.select(tree == 2, values[2], value)
            outgoing(block, slot, link).start()

        each_link(send)

    lag_of = [[LAG * depth(block, tree) for tree in range(TREES)] for block in range(blocks)]
    batches = steps // BATCH
    rest = half - batches * BATCH * span
    padded = cosine.shape[1]

    def cosines(batch):
        for block in range(blocks):
            for piece in range(BATCH * TREES):
                chunk, tree = batch * BATCH + piece // TREES, piece % TREES
                to = (block * BATCH * TREES + piece) * STEP_ROWS
                fresh[to : to + STEP_ROWS] = land[block, tree, chunk + lag_of[block][tree]]
        cosine[...] = lax.dot_general(
            unit[...], fresh[...], (((1,), (1,)), ((), ())), preferred_element_type=jnp.float32
        )

    def cosines_last():
        for block in range(blocks):
            for piece in range(rest // STEP_ROWS):
                chunk, tree = batches * BATCH + piece // TREES, piece % TREES
                to = block * rest + piece * STEP_ROWS
                fresh[to : to + STEP_ROWS] = land[block, tree, chunk + lag_of[block][tree]]
        cosine[:, : blocks * rest] = lax.dot_general(
            unit[...], fresh[: blocks * rest], (((1,), (1,)), ((), ())), preferred_element_type=jnp.float32
        )

    def strips(store, lanes, start, stop):
        pairs = [
            [jnp.concatenate([ref[at : at + 1]] * (lanes // 128), axis=1) for at in (s, s + spreads)]
            for ref in (params_ref, theirs)
            for s in range(spreads)
        ]

        def strip(index, carry):
            rows = pl.ds(pl.multiple_of(index * 16, 16), 16)
            value = cosine[rows, :lanes]
            running = jnp.zeros_like(value)
            for width_of, weight_of in pairs:
                running = running + weight_of * jnp.exp2(width_of * value)
            store(rows, running.astype(jnp.bfloat16))
            return carry

        lax.fori_loop(start // 16, stop // 16, strip, 0)

    def strips_of(batch, start, stop):
        def store(rows, value):
            mine[batch, rows] = value

        strips(store, padded, start, stop)

    def strips_last():
        def store(rows, value):
            mine_last[rows] = value

        strips(store, blocks * rest, 0, row_count)

    def factor_rows(at, batch, side, count):
        for block in range(blocks):
            start = block * block_rows + side * half + batch * BATCH * span
            value = held[pl.ds(pl.multiple_of(start, STEP_ROWS), count)]
            factor[at + block * count : at + (block + 1) * count] = value

    def features_part(left, start, stop):
        def tile_of(tile, carry):
            cols = pl.ds(pl.multiple_of(tile * 512, 512), 512)
            total[:, cols] += jnp.dot(
                left(), factor[:depth_of_left, cols], preferred_element_type=jnp.float32
            )
            return carry

        depth_of_left = 2 * padded
        lax.fori_loop(start, stop, tile_of, 0)

    feature_tiles = feature_count // 512

    def factors(batch):
        factor_rows(0, batch, core, BATCH * span)
        factor_rows(padded, jnp.maximum(batch - 1, 0), 1 - core, BATCH * span)

    def features_of(batch, start, stop):
        features_part(lambda: jnp.concatenate([mine[batch], other[batch]], axis=1), start, stop)

    def unit_piece(index, carry):
        rows = pl.ds(pl.multiple_of(index * 32, 32), 32)
        unit[rows] = normalize(rows_ref[rows].astype(jnp.float32))
        return carry

    for step in range(LAG):
        for block in range(blocks):
            pass_on(block, step, first=True)
    work_from = LAG * deepest + BATCH

    def early(step, carry):
        for block in range(blocks):
            pass_on(block, step)
        for group in range(1, groups):
            pl.when(step == 2 * group)(functools.partial(gather_start, group))
            pl.when(step == 2 * group + 1)(functools.partial(gather_end, group))

        @pl.when(step == 2 * groups)
        def _():
            lax.fori_loop(0, row_count // 32, unit_piece, 0)

        @pl.when(step == 2 * groups + 1)
        def _():
            total[...] = jnp.zeros_like(total)
            other[0] = jnp.zeros_like(other[0])

        return carry

    lax.fori_loop(LAG, work_from, early, 0)
    params_copy.wait()
    whitening_copy.wait()

    def middle(step, carry):
        for block in range(blocks):
            pass_on(block, step)
        batch, part = (step - work_from) // BATCH, (step - work_from) % BATCH

        @pl.when(part == 0)
        def _():
            cosines(batch)
            strips_of(batch, 0, row_count // 3)

        @pl.when(part == 1)
        def _():
            strips_of(batch, row_count // 3, row_count)
            share(batch).start()

        @pl.when(part == 2)
        def _():
            pl.when(batch >= 1)(lambda: share(batch - 1).wait_recv())
            factors(batch)
            features_of(batch, 0, feature_tiles // 2)

        @pl.when(part == 3)
        def _():
            features_of(batch, feature_tiles // 2, feature_tiles)

        return carry

    lax.fori_loop(work_from, rounds - LAG, middle, 0)
    final = batches - 1
    for block in range(blocks):
        pass_on(block, rounds - 2, last=True)
    cosines(final)
    strips_of(final, 0, row_count)
    share(final).start()
    for block in range(blocks):
        pass_on(block, rounds - 1, last=True)
    cosines_last()
    strips_last()
    share_last.start()
    share(final - 1).wait_recv()
    factors(final)
    features_of(final, 0, feature_tiles)
    factor_rows(0, final, 1 - core, BATCH * span)
    factor_rows(padded, batches, core, rest)
    factor_rows(padded + blocks * rest, batches, 1 - core, rest)
    share(final).wait_recv()
    share_last.wait_recv()

    def end_tile(tile, carry):
        cols = pl.ds(pl.multiple_of(tile * 512, 512), 512)
        left = jnp.concatenate([other[batches], mine_last[...], other_last[...]], axis=1)
        added = jnp.dot(left, factor[: padded + 2 * blocks * rest, cols], preferred_element_type=jnp.float32)
        features_ref[:, cols] = (total[:, cols] + added).astype(jnp.bfloat16)
        return carry

    lax.fori_loop(0, feature_tiles, end_tile, 0)
    share_last.wait_send()

    for block in range(blocks):
        for slot in range(2 * LAG):
            each_link(lambda link: outgoing(block, slot, link).wait_send())

    def sent(step, carry):
        share(step).wait_send()
        return carry

    lax.fori_loop(0, batches, sent, 0)


def per_device(
    chips, embeddings, candidates, block_owner, landmark_picks, inverse_width, mixture, whitening
):
    blocks, block_rows = landmark_picks.shape
    row_count, width = embeddings.shape
    feature_count = whitening.shape[1]
    half = block_rows // 2
    span = TREES * STEP_ROWS
    steps = -(-half // span)
    parent_link, depth, leaving = routes(chips.rows, chips.lmks)
    deepest = int(depth.max())
    rounds = steps + LAG * deepest
    batches = steps // BATCH
    rest = half - batches * BATCH * span
    assert steps == batches * BATCH + LAG and rest % 16 == 0
    padded = blocks * BATCH * span
    group_rows = 8 * span
    own_rows = -(-half // group_rows) * group_rows

    first = sum((parent_link[..., t] + 1) << (3 * t) for t in range(TREES))
    first = first + sum(depth[..., t] << (9 + 4 * t) for t in range(TREES))
    second = sum(leaving[..., link] << (2 * link) for link in range(chips.links))
    table = np.stack([first, second], axis=-1).reshape(-1).astype(np.int32)

    slots = (blocks, 2 * LAG, chips.links)
    bf16, f32 = jnp.bfloat16, jnp.float32
    in_vmem = pl.BlockSpec(memory_space=pltpu.VMEM)
    in_smem = pl.BlockSpec(memory_space=pltpu.SMEM)
    return pl.pallas_call(
        functools.partial(fused, chips, rounds, deepest),
        out_shape=jax.ShapeDtypeStruct((row_count, feature_count), bf16),
        in_specs=[in_smem] * 4 + [in_vmem] * 3 + [pl.BlockSpec(memory_space=pl.ANY)],
        out_specs=in_vmem,
        scratch_shapes=[
            pltpu.VMEM((own_rows // STEP_ROWS, STEP_ROWS, width), bf16),
            pltpu.VMEM((blocks, TREES, rounds, STEP_ROWS, width), bf16),
            pltpu.VMEM(slots + (STEP_ROWS, width), bf16),
            pltpu.VMEM(slots + (STEP_ROWS, width), bf16),
            pltpu.VMEM((own_rows, 128), jnp.int32),
            pltpu.VMEM((group_rows, block_rows), bf16),
            pltpu.VMEM((group_rows, width), f32),
            pltpu.VMEM((row_count, width), bf16),
            pltpu.VMEM((padded, width), bf16),
            pltpu.VMEM((row_count, padded), f32),
            pltpu.VMEM((batches, row_count, padded), bf16),
            pltpu.VMEM((batches + 1, row_count, padded), bf16),
            pltpu.VMEM((row_count, blocks * rest), bf16),
            pltpu.VMEM((row_count, blocks * rest), bf16),
            pltpu.VMEM((2 * padded, feature_count), bf16),
            pltpu.VMEM((row_count, feature_count), f32),
            pltpu.VMEM(whitening.shape, bf16),
            pltpu.VMEM((2 * inverse_width.shape[0], 128), f32),
            pltpu.VMEM((2 * inverse_width.shape[0], 128), f32),
            pltpu.SemaphoreType.DMA(slots),
            pltpu.SemaphoreType.DMA(slots),
            pltpu.SemaphoreType.DMA((batches,)),
            pltpu.SemaphoreType.DMA((batches,)),
            pltpu.SemaphoreType.DMA((2,)),
            pltpu.SemaphoreType.DMA((2,)),
            pltpu.SemaphoreType.DMA,
        ],
        compiler_params=pltpu.CompilerParams(
            collective_id=0, has_side_effects=True, vmem_limit_bytes=60 * 1024 * 1024
        ),
        name="fused",
    )(block_owner, jnp.asarray(table), inverse_width, mixture, landmark_picks, embeddings, candidates, whitening)


def solution(mesh):
    chips = Chips(mesh.shape["row"], mesh.shape["lmk"])
    in_specs = (
        P(("row", "lmk"), None),
        P(("row", "lmk"), None),
        P(),
        P(),
        P("bw"),
        P("bw"),
        P(None, "bw"),
    )
    out_specs = P(("row", "lmk"), "bw")
    return jax.shard_map(
        functools.partial(per_device, chips),
        mesh=mesh,
        in_specs=in_specs,
        out_specs=out_specs,
        check_vma=False,
    )
```

```python
import functools
import math
import random

import jax
import jax.numpy as jnp
import numpy as np
from jax import lax
from jax.experimental import pallas as pl
from jax.experimental.pallas import tpu as pltpu
from jax.sharding import PartitionSpec as P

MESH = pl.DeviceIdType.MESH
TREES = 3
STEP_ROWS = 16
LAG = 2
BATCH = 4


class Chips:
    def __init__(self, rows, lmks):
        self.rows, self.lmks = rows, lmks
        self.count = rows * lmks
        self.torus = rows != 4
        if self.torus:
            assert rows == 8 and lmks == 8
            self.back = (1, 0, 3, 2, 5, 4)
        else:
            self.back = (0, 1, 3, 2)
        self.links = len(self.back)

    def neighbour(self, link, row, lmk):
        if not self.torus:
            if link == 0:
                return (row + 2) % 4, lmk
            if link == 1:
                return row + 1 - 2 * (row % 2), lmk
            return row, lmk + (1 if link == 2 else -1)
        x, y, z = row % 4, lmk % 4, (row // 4) * 2 + lmk // 4
        step = 1 if link % 2 == 0 else 3
        if link // 2 == 0:
            x = (x + step) % 4
        elif link // 2 == 1:
            y = (y + step) % 4
        else:
            z = (z + step) % 4
        return (z // 2) * 4 + x, (z % 2) * 4 + y

    def present(self, link, lmk):
        if self.torus or link < 2:
            return None
        return lmk < self.lmks - 1 if link == 2 else lmk > 0

    def degree(self, lmk):
        if self.torus:
            return self.links
        return 2 + jnp.minimum(lmk, 1) + jnp.minimum(self.lmks - 1 - lmk, 1)

    def edges(self, chip):
        row, lmk = chip // self.lmks, chip % self.lmks
        for link in range(self.links):
            here = self.present(link, lmk)
            if here is None or here:
                r, k = self.neighbour(link, row, lmk)
                yield link, r * self.lmks + k


GRID_TREES = [
    [
        [0, 0, 1, 2, 5, 1, 2, 3, 9, 1, 2, 3, 13, 5, 13, 14],
        [0, 9, 10, 11, 12, 13, 14, 15, 0, 8, 9, 10, 8, 9, 10, 11],
        [0, 5, 6, 7, 0, 4, 5, 6, 12, 13, 14, 15, 4, 12, 6, 7],
    ],
    [
        [1, 1, 1, 2, 0, 4, 2, 3, 0, 10, 2, 3, 8, 14, 6, 7],
        [4, 1, 6, 7, 5, 1, 5, 6, 12, 13, 14, 15, 4, 5, 13, 14],
        [8, 1, 10, 11, 12, 13, 14, 15, 9, 1, 9, 10, 13, 9, 10, 11],
    ],
]


def torus_trees(chips):
    for seed in range(1000):
        draw = random.Random(seed)
        used, trees = set(), []
        for tree in range(TREES):
            parent, level = {0: 0}, [0]
            while level:
                following = []
                draw.shuffle(level)
                for chip in level:
                    for link, other in chips.edges(chip):
                        if other in parent or (chip, link) in used:
                            continue
                        if chip == 0 and link // 2 != tree:
                            continue
                        used.add((chip, link))
                        parent[other] = chip
                        following.append(other)
                level = following
            trees.append(parent)
        if all(len(parent) == chips.count for parent in trees):
            return [[parent[chip] for chip in range(chips.count)] for parent in trees]
    raise ValueError("no trees")


def moved(chips, owner):
    if not chips.torus:
        y, x, z = owner // 8, owner // 4 % 2, owner % 4
        turn = z >= 2
        image = [
            ((c // 8) ^ y) * 8 + ((c // 4 % 2) ^ x) * 4 + (3 - c % 4 if turn else c % 4)
            for c in range(16)
        ]
        return image, (3 - z if turn else z)

    def place(chip):
        row, lmk = chip // 8, chip % 8
        return row % 4, lmk % 4, (row // 4) * 2 + lmk // 4

    away = place(owner)
    image = []
    for chip in range(chips.count):
        x, y, z = ((a + b) % 4 for a, b in zip(place(chip), away))
        image.append(((z // 2) * 4 + x) * 8 + (z % 2) * 4 + y)
    return image, 0


@functools.lru_cache(maxsize=None)
def routes(rows, lmks):
    chips = Chips(rows, lmks)
    stored = [torus_trees(chips)] if chips.torus else GRID_TREES
    n = chips.count
    parent_link = np.full((n, n, TREES), -1, np.int32)
    depth = np.zeros((n, n, TREES), np.int32)
    leaving = np.full((n, n, chips.links), 3, np.int32)
    for owner in range(n):
        image, root = moved(chips, owner)
        for tree in range(TREES):
            parent = [0] * n
            for chip in range(n):
                parent[image[chip]] = image[stored[root][tree][chip]]
            for chip in range(n):
                if chip == owner:
                    continue
                for link, other in chips.edges(parent[chip]):
                    if other == chip:
                        leaving[owner, parent[chip], link] = tree
                        parent_link[owner, chip, tree] = chips.back[link]
                        break
                at = chip
                while at != owner:
                    at = parent[at]
                    depth[owner, chip, tree] += 1
    return parent_link, depth, leaving


def fused(
    chips, rounds, deepest, fixed_words,
    owner_ref, table_ref, widths_ref, weights_ref, picks_ref, rows_ref, candidates_ref, whitening_ref,
    features_ref,
    own, fixed, land, arrive, leave, columns, places, product, unit, fresh, cosine, mine, other, mine_last, other_last, factor, total, held, params_ref, theirs,
    fixed_send_sem, fixed_sem, send_sem, recv_sem, mine_sem, other_sem, last_sem, params_sem, held_sem,
):
    row, lmk, core = lax.axis_index("row"), lax.axis_index("lmk"), lax.axis_index("bw")
    me = row * chips.lmks + lmk
    blocks = owner_ref.shape[0]
    last_chip = chips.count - 1
    block_rows, width = candidates_ref.shape
    half = block_rows // 2
    row_count, feature_count = total.shape
    span = TREES * STEP_ROWS
    steps = -(-half // span)
    partner = {"bw": 1 - core}

    def each_link(act):
        for link in range(chips.links):
            here = chips.present(link, lmk)
            if here is None:
                act(link)
            else:
                pl.when(here)(functools.partial(act, link))

    def target(link):
        r, k = chips.neighbour(link, row, lmk)
        return {"row": r, "lmk": k}

    def copy_to(link, slot, arriving):
        return pltpu.make_async_remote_copy(
            src_ref=leave.at[slot, link],
            dst_ref=arrive.at[slot, arriving],
            send_sem=send_sem.at[slot, link],
            recv_sem=recv_sem.at[slot, arriving],
            device_id=target(link),
            device_id_type=MESH,
        )

    def outgoing(slot, link):
        return copy_to(link, slot, chips.back[link])

    def incoming(slot, link):
        return copy_to(link, slot, link)

    def fixed_copy(link, tree, chunk):
        return pltpu.make_async_remote_copy(
            src_ref=fixed.at[tree, chunk],
            dst_ref=fixed.at[tree, chunk],
            send_sem=fixed_send_sem.at[link, chunk % 4],
            recv_sem=fixed_sem.at[tree, chunk],
            device_id=target(link),
            device_id_type=MESH,
        )

    def share(step):
        return pltpu.make_async_remote_copy(
            src_ref=mine.at[step],
            dst_ref=other.at[step + 1],
            send_sem=mine_sem.at[step],
            recv_sem=other_sem.at[step],
            device_id=partner,
            device_id_type=MESH,
        )

    share_last = pltpu.make_async_remote_copy(
        src_ref=mine_last,
        dst_ref=other_last,
        send_sem=last_sem.at[0],
        recv_sem=last_sem.at[1],
        device_id=partner,
        device_id_type=MESH,
    )
    params_copy = pltpu.make_async_remote_copy(
        src_ref=params_ref,
        dst_ref=theirs,
        send_sem=params_sem.at[0],
        recv_sem=params_sem.at[1],
        device_id=partner,
        device_id_type=MESH,
    )
    whitening_copy = pltpu.make_async_copy(whitening_ref, held, held_sem)

    barrier = pltpu.get_barrier_semaphore()

    def greet(link):
        pl.semaphore_signal(barrier, inc=1, device_id=target(link), device_id_type=MESH)

    each_link(greet)
    pl.semaphore_signal(barrier, inc=1, device_id=partner, device_id_type=MESH)
    whitening_copy.start()

    last_block = (owner_ref[1] == last_chip).astype(jnp.int32)
    stream_block = [last_block, 1 - last_block]
    other_owner = jnp.where(last_block == 1, owner_ref[0], owner_ref[1])
    at = 2 * (other_owner * chips.count + me)
    flood_words = table_ref[at], table_ref[at + 1]
    def is_equal(a, b):
        return 1 - jnp.minimum(jnp.maximum(a - b, b - a), 1)

    place_words = [
        sum(is_equal(me, chip) * word for chip, word in enumerate(words)) for words in fixed_words
    ]

    def parent(words, tree):
        return (words[0] // 8**tree) % 8

    def depth(words, tree):
        return (words[0] // (512 * 16**tree)) % 16

    def leaving(words, link):
        return (words[1] // 4**link) % 4

    fixed_depth = [depth(place_words, tree) for tree in range(TREES)]
    fixed_leaving = [leaving(place_words, link) for link in range(chips.links)]

    for group in range(half // 128):
        lanes_of = pl.ds(pl.multiple_of(core * half + group * 128, 128), 128)
        wanted_block = jnp.where(me == last_chip, stream_block[0], stream_block[1])
        picked = lax.select(wanted_block == 1, picks_ref[1:2, lanes_of], picks_ref[0:1, lanes_of])
        columns[group * 128 : (group + 1) * 128] = jnp.transpose(jnp.broadcast_to(picked, (128, 128)))
    columns[half:] = jnp.zeros_like(columns[half:])

    def normalize(widened):
        scale = lax.rsqrt(jnp.sum(widened * widened, axis=-1, keepdims=True) + 1e-06)
        return (widened * scale).astype(jnp.bfloat16)

    def products(first_tile, last_tile):
        def tile_of(tile, carry):
            cols = pl.ds(pl.multiple_of(tile * 256, 256), 256)
            product[:, cols] = jnp.dot(
                places[...], candidates_ref[:, cols], preferred_element_type=jnp.float32
            )
            return carry

        lax.fori_loop(first_tile, last_tile, tile_of, 0)

    tiles = width // 256

    def gather_start(group):
        size = places.shape[0]
        lanes = lax.broadcasted_iota(jnp.int32, (size, 128), 1)
        wanted = columns[group * size : (group + 1) * size]
        for tile in range(block_rows // 128):
            places[:, tile * 128 : (tile + 1) * 128] = jnp.where(
                wanted == lanes + tile * 128, 1.0, 0.0
            ).astype(jnp.bfloat16)
        products(0, tiles // 2)

    def gather_end(group):
        products(tiles // 2, tiles)
        pieces = places.shape[0] // STEP_ROWS

        def piece(index, carry):
            rows = pl.ds(pl.multiple_of(index * STEP_ROWS, STEP_ROWS), STEP_ROWS)
            own[group * pieces + index] = normalize(product[rows])
            return carry

        lax.fori_loop(0, pieces, piece, 0)

    spreads = widths_ref.shape[0]
    for s in range(spreads):
        params_ref[s : s + 1] = jnp.full((1, 128), widths_ref[s] * (2.0 * math.log2(math.e)), jnp.float32)
        params_ref[spreads + s : spreads + s + 1] = jnp.full((1, 128), weights_ref[s], jnp.float32)

    groups = own.shape[0] * STEP_ROWS // places.shape[0]
    gather_start(0)
    gather_end(0)
    pl.semaphore_wait(barrier, chips.degree(lmk) + 1)
    params_copy.start()

    def relay(step):
        for tree in range(TREES):
            chunk = step - LAG * fixed_depth[tree]
            live = jnp.logical_and(chunk >= 0, chunk < steps)

            @pl.when(jnp.logical_and(live, me == last_chip))
            def _():
                fixed[tree, chunk] = own[chunk * TREES + tree]

            @pl.when(jnp.logical_and(live, me != last_chip))
            def _():
                fixed_copy(0, tree, chunk).wait_recv()

        for link in range(chips.links):
            tree = fixed_leaving[link]
            chunk = step - LAG * sum(is_equal(tree, t) * fixed_depth[t] for t in range(TREES))
            live = jnp.logical_and(chunk >= 0, chunk < steps)

            @pl.when(jnp.logical_and(live, tree < TREES))
            def _():
                @pl.when(chunk >= 4)
                def _():
                    fixed_copy(link, tree, chunk).wait_send()

                fixed_copy(link, tree, chunk).start()

    def pass_on(step, first=False, last=False):
        slot, before = step % (2 * LAG), (step + LAG) % (2 * LAG)
        if not first:
            each_link(lambda link: incoming(before, link).wait_recv())
        values = []
        for tree in range(TREES):
            origin = parent(flood_words, tree)
            value = own[jnp.minimum(step, steps - 1) * TREES + tree]
            if not first:
                for link in range(chips.links):
                    value = lax.select(origin == link + 1, arrive[before, link], value)
            land[tree, step] = value
            values.append(value)
        if last:
            return

        def send(link):
            if not first:

                @pl.when(step >= 2 * LAG)
                def _():
                    outgoing(slot, link).wait_send()

            tree = leaving(flood_words, link)
            value = lax.select(tree == 1, values[1], values[0])
            leave[slot, link] = lax.select(tree == 2, values[2], value)
            outgoing(slot, link).start()

        each_link(send)

    def one_round(step, first=False, last=False):
        relay(step)
        pass_on(step, first, last)

    lag_of = [LAG * depth(flood_words, tree) for tree in range(TREES)]

    def landed(stream, tree, chunk):
        return fixed[tree, chunk] if stream == 0 else land[tree, chunk + lag_of[tree]]

    batches = steps // BATCH
    rest = half - batches * BATCH * span
    padded = cosine.shape[1]

    def cosines(batch):
        for block in range(blocks):
            for piece in range(BATCH * TREES):
                chunk, tree = batch * BATCH + piece // TREES, piece % TREES
                to = (block * BATCH * TREES + piece) * STEP_ROWS
                fresh[to : to + STEP_ROWS] = landed(block, tree, chunk)
        cosine[...] = lax.dot_general(
            unit[...], fresh[...], (((1,), (1,)), ((), ())), preferred_element_type=jnp.float32
        )

    def cosines_last():
        for block in range(blocks):
            for piece in range(rest // STEP_ROWS):
                chunk, tree = batches * BATCH + piece // TREES, piece % TREES
                to = block * rest + piece * STEP_ROWS
                fresh[to : to + STEP_ROWS] = landed(block, tree, chunk)
        cosine[:, : blocks * rest] = lax.dot_general(
            unit[...], fresh[: blocks * rest], (((1,), (1,)), ((), ())), preferred_element_type=jnp.float32
        )

    def strips(store, lanes, start, stop):
        pairs = [
            [jnp.concatenate([ref[at : at + 1]] * (lanes // 128), axis=1) for at in (s, s + spreads)]
            for ref in (params_ref, theirs)
            for s in range(spreads)
        ]

        def strip(index, carry):
            rows = pl.ds(pl.multiple_of(index * 16, 16), 16)
            value = cosine[rows, :lanes]
            running = jnp.zeros_like(value)
            for width_of, weight_of in pairs:
                running = running + weight_of * jnp.exp2(width_of * value)
            store(rows, running.astype(jnp.bfloat16))
            return carry

        lax.fori_loop(start // 16, stop // 16, strip, 0)

    def strips_of(batch, start, stop):
        def store(rows, value):
            mine[batch, rows] = value

        strips(store, padded, start, stop)

    def strips_last():
        def store(rows, value):
            mine_last[rows] = value

        strips(store, blocks * rest, 0, row_count)

    def factor_rows(at, batch, side, count):
        for block in range(blocks):
            start = side * half + batch * BATCH * span
            value = lax.select(
                stream_block[block] == 1,
                held[pl.ds(pl.multiple_of(start + block_rows, STEP_ROWS), count)],
                held[pl.ds(pl.multiple_of(start, STEP_ROWS), count)],
            )
            factor[at + block * count : at + (block + 1) * count] = value

    def features_part(left, start, stop):
        def tile_of(tile, carry):
            cols = pl.ds(pl.multiple_of(tile * 512, 512), 512)
            total[:, cols] += jnp.dot(
                left(), factor[:depth_of_left, cols], preferred_element_type=jnp.float32
            )
            return carry

        depth_of_left = 2 * padded
        lax.fori_loop(start, stop, tile_of, 0)

    feature_tiles = feature_count // 512

    def factors(batch):
        factor_rows(0, batch, core, BATCH * span)
        factor_rows(padded, jnp.maximum(batch - 1, 0), 1 - core, BATCH * span)

    def features_of(batch, start, stop):
        features_part(lambda: jnp.concatenate([mine[batch], other[batch]], axis=1), start, stop)

    def unit_piece(index, carry):
        rows = pl.ds(pl.multiple_of(index * 32, 32), 32)
        unit[rows] = normalize(rows_ref[rows].astype(jnp.float32))
        return carry

    for step in range(LAG):
        one_round(step, first=True)
    work_from = LAG * deepest + BATCH

    def early(step, carry):
        one_round(step)
        for group in range(1, groups):
            pl.when(step == 2 * group)(functools.partial(gather_start, group))
            pl.when(step == 2 * group + 1)(functools.partial(gather_end, group))

        @pl.when(step == 2 * groups)
        def _():
            lax.fori_loop(0, row_count // 32, unit_piece, 0)

        @pl.when(step == 2 * groups + 1)
        def _():
            total[...] = jnp.zeros_like(total)
            other[0] = jnp.zeros_like(other[0])

        return carry

    lax.fori_loop(LAG, work_from, early, 0)
    params_copy.wait()
    whitening_copy.wait()

    def middle(step, carry):
        one_round(step)
        batch, part = (step - work_from) // BATCH, (step - work_from) % BATCH

        @pl.when(part == 0)
        def _():
            cosines(batch)
            strips_of(batch, 0, row_count // 3)

        @pl.when(part == 1)
        def _():
            strips_of(batch, row_count // 3, row_count)
            share(batch).start()

        @pl.when(part == 2)
        def _():
            pl.when(batch >= 1)(lambda: share(batch - 1).wait_recv())
            factors(batch)
            features_of(batch, 0, feature_tiles // 2)

        @pl.when(part == 3)
        def _():
            features_of(batch, feature_tiles // 2, feature_tiles)

        return carry

    lax.fori_loop(work_from, rounds - LAG, middle, 0)
    final = batches - 1
    one_round(rounds - 2, last=True)
    cosines(final)
    strips_of(final, 0, row_count)
    share(final).start()
    one_round(rounds - 1, last=True)
    cosines_last()
    strips_last()
    share_last.start()
    share(final - 1).wait_recv()
    factors(final)
    features_of(final, 0, feature_tiles)
    factor_rows(0, final, 1 - core, BATCH * span)
    factor_rows(padded, batches, core, rest)
    factor_rows(padded + blocks * rest, batches, 1 - core, rest)
    share(final).wait_recv()
    share_last.wait_recv()

    def end_tile(tile, carry):
        cols = pl.ds(pl.multiple_of(tile * 512, 512), 512)
        left = jnp.concatenate([other[batches], mine_last[...], other_last[...]], axis=1)
        added = jnp.dot(left, factor[: padded + 2 * blocks * rest, cols], preferred_element_type=jnp.float32)
        features_ref[:, cols] = (total[:, cols] + added).astype(jnp.bfloat16)
        return carry

    lax.fori_loop(0, feature_tiles, end_tile, 0)
    share_last.wait_send()

    for slot in range(2 * LAG):
        each_link(lambda link: outgoing(slot, link).wait_send())
    for link in range(chips.links):

        @pl.when(fixed_leaving[link] < TREES)
        def _():
            for chunk in range(steps - 4, steps):
                fixed_copy(link, fixed_leaving[link], chunk).wait_send()

    def sent(step, carry):
        share(step).wait_send()
        return carry

    lax.fori_loop(0, batches, sent, 0)


def per_device(
    chips, embeddings, candidates, block_owner, landmark_picks, inverse_width, mixture, whitening
):
    blocks, block_rows = landmark_picks.shape
    row_count, width = embeddings.shape
    feature_count = whitening.shape[1]
    half = block_rows // 2
    span = TREES * STEP_ROWS
    steps = -(-half // span)
    parent_link, depth, leaving = routes(chips.rows, chips.lmks)
    deepest = int(depth.max())
    rounds = steps + LAG * deepest
    batches = steps // BATCH
    rest = half - batches * BATCH * span
    assert steps == batches * BATCH + LAG and rest % 16 == 0
    padded = blocks * BATCH * span
    group_rows = 8 * span
    own_rows = -(-half // group_rows) * group_rows

    first = sum((parent_link[..., t] + 1) << (3 * t) for t in range(TREES))
    first = first + sum(depth[..., t] << (9 + 4 * t) for t in range(TREES))
    second = sum(leaving[..., link] << (2 * link) for link in range(chips.links))
    table = np.stack([first, second], axis=-1).reshape(-1).astype(np.int32)
    fixed_words = [[int(word) for word in words[chips.count - 1]] for words in (first, second)]

    slots = (2 * LAG, chips.links)
    bf16, f32 = jnp.bfloat16, jnp.float32
    in_vmem = pl.BlockSpec(memory_space=pltpu.VMEM)
    in_smem = pl.BlockSpec(memory_space=pltpu.SMEM)
    return pl.pallas_call(
        functools.partial(fused, chips, rounds, deepest, fixed_words),
        out_shape=jax.ShapeDtypeStruct((row_count, feature_count), bf16),
        in_specs=[in_smem] * 4 + [in_vmem] * 3 + [pl.BlockSpec(memory_space=pl.ANY)],
        out_specs=in_vmem,
        scratch_shapes=[
            pltpu.VMEM((own_rows // STEP_ROWS, STEP_ROWS, width), bf16),
            pltpu.VMEM((TREES, steps, STEP_ROWS, width), bf16),
            pltpu.VMEM((TREES, rounds, STEP_ROWS, width), bf16),
            pltpu.VMEM(slots + (STEP_ROWS, width), bf16),
            pltpu.VMEM(slots + (STEP_ROWS, width), bf16),
            pltpu.VMEM((own_rows, 128), jnp.int32),
            pltpu.VMEM((group_rows, block_rows), bf16),
            pltpu.VMEM((group_rows, width), f32),
            pltpu.VMEM((row_count, width), bf16),
            pltpu.VMEM((padded, width), bf16),
            pltpu.VMEM((row_count, padded), f32),
            pltpu.VMEM((batches, row_count, padded), bf16),
            pltpu.VMEM((batches + 1, row_count, padded), bf16),
            pltpu.VMEM((row_count, blocks * rest), bf16),
            pltpu.VMEM((row_count, blocks * rest), bf16),
            pltpu.VMEM((2 * padded, feature_count), bf16),
            pltpu.VMEM((row_count, feature_count), f32),
            pltpu.VMEM(whitening.shape, bf16),
            pltpu.VMEM((2 * inverse_width.shape[0], 128), f32),
            pltpu.VMEM((2 * inverse_width.shape[0], 128), f32),
            pltpu.SemaphoreType.DMA((chips.links, 4)),
            pltpu.SemaphoreType.DMA((TREES, steps)),
            pltpu.SemaphoreType.DMA(slots),
            pltpu.SemaphoreType.DMA(slots),
            pltpu.SemaphoreType.DMA((batches,)),
            pltpu.SemaphoreType.DMA((batches,)),
            pltpu.SemaphoreType.DMA((2,)),
            pltpu.SemaphoreType.DMA((2,)),
            pltpu.SemaphoreType.DMA,
        ],
        compiler_params=pltpu.CompilerParams(
            collective_id=0, has_side_effects=True, vmem_limit_bytes=60 * 1024 * 1024
        ),
        name="fused",
    )(block_owner, jnp.asarray(table), inverse_width, mixture, landmark_picks, embeddings, candidates, whitening)


def solution(mesh):
    chips = Chips(mesh.shape["row"], mesh.shape["lmk"])
    in_specs = (
        P(("row", "lmk"), None),
        P(("row", "lmk"), None),
        P(),
        P(),
        P("bw"),
        P("bw"),
        P(None, "bw"),
    )
    out_specs = P(("row", "lmk"), "bw")
    return jax.shard_map(
        functools.partial(per_device, chips),
        mesh=mesh,
        in_specs=in_specs,
        out_specs=out_specs,
        check_vma=False,
    )
```
